128 devices in a mesh: tm: 2 (over y_hi), tile: 64 (over z, y_lo, x, core).
Axes of the slice: x: 4, y: 4 (y_hi: 2, y_lo: 2; y = y_hi * 2 + y_lo), z: 4, core: 2. Of those that a mesh axis runs over, the one named last changes fastest.
Arguments:
- latent: bfloat16 [2, 192, 512, 256], P('tm', None, 'tile'), may hold values from -200 to 200, as said below
- coarse_cache: bfloat16 [2, 192, 512, 256], P('tm', None, 'tile'), may hold values from -6 to 6
- fine_cache: bfloat16 [2, 96, 1024, 512], P('tm', None, 'tile'), may hold values from -6 to 6
- gain_coarse: float32 [192], replicated, may hold values from 0.1 to 1.9
- shift_coarse: float32 [192], replicated, may hold values from -3 to 3
- weight_coarse: bfloat16 [3, 3, 3, 192, 192], replicated, may hold values from -0.078125 to 0.078125
- weight_up: bfloat16 [3, 3, 96, 192], replicated, may hold values from -0.15625 to 0.15625
- gain_fine: float32 [96], replicated, may hold values from 0.1 to 1.9
- shift_fine: float32 [96], replicated, may hold values from -3 to 3
- weight_fine: bfloat16 [3, 3, 3, 96, 96], replicated, may hold values from -0.125 to 0.125
- bias_fine: float32 [96], replicated, may hold values from -3 to 3
Outputs:
- decoded: bfloat16 [2, 96, 1024, 512], P('tm', None, 'tile')
The draws below stay inside these ranges and needn't reach their ends.
Inputs may be any that keep to these rules, and one draw needn't show every extreme that they name: `latent`: the coarse block's input before its norm.
All inputs are finite; a program needn't handle non-finite values.
Results may differ from the reference program's by a relative error of at most 0.0046.
Values may be sent and summed in bfloat16 or wider, within the bound.
No kernel may reach another device: no remote copies, remote signals or barrier semaphores. Data moves between devices by JAX's collectives and lax.ppermute only.
A program may use at most 256 MiB of HBM per device.

```python
import jax
import jax.numpy as jnp
from jax import lax

C1 = 192
C2 = 96
GROUPS = 32
COLS = 256
FRAMES = 2
H1 = 512
H2 = 1024


def draw_latent(key, part):
    key = jax.random.fold_in(key, 7)
    key_noise, key_row, key_col = jax.random.split(key, 3)
    ramp = 3.0 ** (jnp.arange(H1, dtype=jnp.float32) / (H1 - 1))
    values = jnp.clip(jax.random.normal(key_noise, (FRAMES, C1, H1, COLS), jnp.float32), -6.0, 6.0)
    row_scale = 10.0 ** jax.random.uniform(key_row, (H1,), jnp.float32, 0.0, 1.0)
    col_scale = 10.0 ** jax.random.uniform(key_col, (COLS,), jnp.float32, 0.0, 1.0)
    scale = 0.1 * (ramp * row_scale)[:, None] * col_scale[None, :]
    return (values * scale[None, None]).astype(jnp.bfloat16)


def steps_of(stream_key, dims, cuts, low, high):
    def one(axis_at, blocks):
        heights = jax.random.uniform(jax.random.fold_in(jax.random.fold_in(stream_key, 6), axis_at), (blocks,), jnp.float32, low / len(cuts), high / len(cuts))
        return jnp.repeat(jnp.exp(heights), dims[axis_at] // blocks).reshape((-1,) + (1,) * (len(dims) - axis_at - 1))

    loudness = one(*cuts[0])
    for cut in cuts[1:]:
        loudness = loudness * one(*cut)
    return loudness


def normal_values(own_key, shape, width, most, cuts=(), held_as=jnp.bfloat16):
    values = width * jax.random.normal(own_key, shape, jnp.float32)
    if cuts:
        values = values * steps_of(own_key, shape, cuts, -0.22, 0.18)
    return jnp.clip(values, -most, most).astype(held_as)


def setup_inputs(seed: int = 0) -> dict:
    key_list = jax.random.split(jax.random.key(seed), 12)
    latent = draw_latent(jax.random.fold_in(key_list[11], 71), 0)
    coarse_cache = normal_values(key_list[1], (2, C1, H1, COLS), 1.0, 6.0, ((0, 2), (2, 64)))
    fine_cache = normal_values(key_list[2], (2, C2, H2, 2 * COLS), 1.0, 6.0, ((0, 2), (2, 64)))
    gain_coarse = jnp.clip(1.0 + 0.18 * jax.random.normal(key_list[3], (C1,), jnp.float32), 0.1, 1.9)
    shift_coarse = normal_values(key_list[4], (C1,), 0.5, 3.0, (), jnp.float32)
    weight_coarse = normal_values(key_list[5], (3, 3, 3, C1, C1), (27 * C1) ** -0.5, 0.078125)
    weight_up = normal_values(key_list[6], (3, 3, C2, C1), (9 * C1) ** -0.5, 0.15625)
    gain_fine = jnp.clip(1.0 + 0.18 * jax.random.normal(key_list[7], (C2,), jnp.float32), 0.1, 1.9)
    shift_fine = normal_values(key_list[8], (C2,), 0.5, 3.0, (), jnp.float32)
    weight_fine = normal_values(key_list[9], (3, 3, 3, C2, C2), (27 * C2) ** -0.5, 0.125)
    bias_fine = normal_values(key_list[10], (C2,), 0.5, 3.0, (), jnp.float32)
    return dict(latent=latent, coarse_cache=coarse_cache, fine_cache=fine_cache, gain_coarse=gain_coarse, shift_coarse=shift_coarse, weight_coarse=weight_coarse, weight_up=weight_up, gain_fine=gain_fine, shift_fine=shift_fine, weight_fine=weight_fine, bias_fine=bias_fine)


EPS = 1e-05

def group_moments(frame_data):
    grouped = frame_data.astype(jnp.float32).reshape(GROUPS, -1)
    centre = lax.optimization_barrier(jnp.mean(grouped, axis=1))
    centred = grouped - centre[:, None]
    spread = lax.rsqrt(lax.optimization_barrier(jnp.mean(centred * centred, axis=1)) + EPS)
    return (centre, spread)

def activate(frame_data, centre, spread, gain, shift):
    channels = frame_data.shape[0]
    centre_full = jnp.repeat(centre, channels // GROUPS)[:, None, None]
    spread_full = jnp.repeat(spread, channels // GROUPS)[:, None, None]
    value = (frame_data.astype(jnp.float32) - centre_full) * spread_full * gain[:, None, None] + shift[:, None, None]
    return jax.nn.silu(value).astype(jnp.bfloat16)

def conv_frames(padded, weight, out_rows, out_cols):
    summed = jnp.zeros((weight.shape[3], out_rows, out_cols), jnp.float32)
    for time_tap in range(3):
        for row_tap in range(3):
            for col_tap in range(3):
                window = padded[time_tap, :, row_tap:row_tap + out_rows, col_tap:col_tap + out_cols]
                summed = summed + jnp.einsum('oc,crw->orw', weight[time_tap, row_tap, col_tap].astype(jnp.float32), window.astype(jnp.float32), precision=lax.Precision.HIGHEST)
    return summed

def conv_plane(padded, weight, out_rows, out_cols):
    summed = jnp.zeros((weight.shape[2], out_rows, out_cols), jnp.float32)
    for row_tap in range(3):
        for col_tap in range(3):
            window = padded[:, row_tap:row_tap + out_rows, col_tap:col_tap + out_cols]
            summed = summed + jnp.einsum('oc,crw->orw', weight[row_tap, col_tap].astype(jnp.float32), window.astype(jnp.float32), precision=lax.Precision.HIGHEST)
    return summed

def reference(latent, coarse_cache, fine_cache, gain_coarse, shift_coarse, weight_coarse, weight_up, gain_fine, shift_fine, weight_fine, bias_fine):
    height = latent.shape[2]
    across = latent.shape[3]
    actives = []
    for frame in range(FRAMES):
        centre, spread = group_moments(latent[frame])
        actives.append(activate(latent[frame], centre, spread, gain_coarse, shift_coarse))
    sequence = jnp.concatenate([coarse_cache, jnp.stack(actives)], axis=0)
    fine_actives = []
    for frame in range(FRAMES):
        padded = jnp.pad(sequence[frame:frame + 3], ((0, 0), (0, 0), (1, 1), (1, 1)))
        coarse = conv_frames(padded, weight_coarse, height, across).astype(jnp.bfloat16)
        upsampled = jnp.repeat(jnp.repeat(coarse, 2, axis=1), 2, axis=2)
        upsampled = jnp.pad(upsampled, ((0, 0), (1, 1), (1, 1)))
        raised = conv_plane(upsampled, weight_up, 2 * height, 2 * across).astype(jnp.bfloat16)
        centre, spread = group_moments(raised)
        fine_actives.append(activate(raised, centre, spread, gain_fine, shift_fine))
    fine_sequence = jnp.concatenate([fine_cache, jnp.stack(fine_actives)], axis=0)
    outputs = []
    for frame in range(FRAMES):
        padded = jnp.pad(fine_sequence[frame:frame + 3], ((0, 0), (0, 0), (1, 1), (1, 1)))
        result = conv_frames(padded, weight_fine, 2 * height, 2 * across) + bias_fine[:, None, None]
        outputs.append(result.astype(jnp.bfloat16))
    return jnp.stack(outputs)
```

```python
import jax
import jax.numpy as jnp
from jax import lax
from jax.experimental import pallas as pl
from jax.experimental.pallas import tpu as pltpu
from jax.sharding import PartitionSpec as P

GROUPS = 32
EPS = 1e-05
f32 = jnp.float32
bf16 = jnp.bfloat16


def call(kernel, name, outs, scratch=()):
    return pl.pallas_call(
        kernel,
        out_shape=[jax.ShapeDtypeStruct(s, d) for s, d in outs],
        scratch_shapes=list(scratch),
        compiler_params=pltpu.CompilerParams(vmem_limit_bytes=56 * 2**20),
        name=name,
    )


def dot(a, b):
    return jnp.dot(a, b, preferred_element_type=f32)


def moments(rows, count):
    total = rows[0].astype(f32)
    for row in rows[1:]:
        total = total + row.astype(f32)
    mean = jnp.sum(total, axis=1, keepdims=True) / count
    squares = None
    for row in rows:
        centred = row.astype(f32) - mean
        squares = centred * centred if squares is None else squares + centred * centred
    return mean, jnp.sum(squares, axis=1, keepdims=True)


def payload(ref, mean, squares):
    channels = mean.shape[0]
    lane = lax.broadcasted_iota(jnp.int32, (channels, 128), 1)
    turned = jnp.transpose(jnp.where(lane == 0, mean, squares))
    half = ref.shape[1] // 2
    ref[...] = jnp.zeros(ref.shape, f32)
    ref[:, :channels] = jnp.broadcast_to(turned[0:1], (ref.shape[0], channels))
    ref[:, half : half + channels] = jnp.broadcast_to(turned[1:2], (ref.shape[0], channels))


def combine(stats, channels, per_device):
    devices, width = stats.shape
    half = width // 2
    turned = jnp.transpose(stats)
    mean = turned[:channels]
    squares = turned[half : half + channels]
    size = channels // GROUPS
    row = lax.broadcasted_iota(jnp.int32, (channels, channels), 0) // size
    col = lax.broadcasted_iota(jnp.int32, (channels, channels), 1) // size
    same = (row == col).astype(f32)

    def group_sum(column):
        wide = jnp.broadcast_to(column, (channels, 128))
        return jnp.dot(
            same, wide, preferred_element_type=f32, precision=lax.Precision.HIGHEST
        )[:, :1]

    centre = group_sum(jnp.sum(mean, axis=1, keepdims=True)) / (devices * size)
    away = mean - centre
    total = jnp.sum(squares + per_device * (away * away), axis=1, keepdims=True)
    variance = group_sum(total) / (devices * size * per_device)
    return centre, lax.rsqrt(variance + EPS)


def silu_norm(x, centre, scale, shift):
    half = 0.5 * ((x.astype(f32) - centre) * scale + shift)
    return half + half * jnp.tanh(half)


def put(ref, slot, row, x):
    channels, width = x.shape
    lane = lax.broadcasted_iota(jnp.int32, (channels, width), 1)
    wide = x.astype(f32)
    left = jnp.where(lane == 0, 0.0, pltpu.roll(wide, 1, 1))
    right = jnp.where(lane == width - 1, 0.0, pltpu.roll(wide, width - 1, 1))
    base = row * 3 * channels
    ref[slot, base : base + channels] = left.astype(bf16)
    ref[slot, base + channels : base + 2 * channels] = x.astype(bf16)
    ref[slot, base + 2 * channels : base + 3 * channels] = right.astype(bf16)


def weights_kernel(coarse, up, fine, out_coarse, out_up, out_fine):
    c1, c2 = coarse.shape[3], fine.shape[3]
    for t in range(3):
        for a in range(3):
            for b in range(3):
                at = (a * 3 + b) * c1
                out_coarse[t, :, at : at + c1] = coarse[t, a, b]
    for b in range(3):
        first, second, third = (up[a, b].astype(f32) for a in range(3))
        at = b * c1
        for rows, a, value in (
            (0, 0, first + second),
            (0, 1, third),
            (1, 0, first),
            (1, 1, second + third),
        ):
            out_up[rows * c2 : (rows + 1) * c2, a * 3 * c1 + at : a * 3 * c1 + at + c1] = (
                value.astype(bf16)
            )
    out_fine[...] = jnp.zeros(out_fine.shape, bf16)
    for t in range(3):
        for a in range(3):
            for b in range(3):
                block = fine[t, a, b]
                for rho in range(2):
                    at = ((a + rho) * 3 + b) * c2
                    out_fine[t, rho * c2 : (rho + 1) * c2, at : at + c2] = block


def first_kernel(latent, cache, fine, lat_t, cache_t, fine_t, send, up, down, pay):
    frame = lax.axis_index("tm")
    rows = latent.shape[1]
    lat = jnp.swapaxes(latent[...], 0, 1)
    lat_t[...] = lat
    cac = jnp.swapaxes(cache[...], 0, 1)
    cache_t[...] = cac
    fin = jnp.swapaxes(fine[...], 0, 1)
    fine_t[...] = fin

    @pl.when(frame == 0)
    def _():
        send[...] = lat_t[...]

    @pl.when(frame != 0)
    def _():
        send[...] = cache_t[...]

    c2, half = fine.shape[0], latent.shape[2]
    for ref, cut, edge in ((up, slice(rows - 2, rows), 2 * rows - 1), (down, slice(0, 2), 0)):
        ref[0:2] = lat_t[cut]
        ref[2:4] = cache_t[cut]
        ref[4, :c2] = fine_t[edge, :, :half]
        ref[4, c2:] = fine_t[edge, :, half:]
    payload(pay, *moments([lat_t[r] for r in range(rows)], rows * latent.shape[2]))


def conv_coarse_a(lat_t, cache_t, above, below, stats, gain, weights, acc, stack):
    tile = lax.axis_index("tile")
    last = lax.axis_size("tile") - 1
    rows, channels, width = lat_t.shape
    centre, spread = combine(stats[...], channels, rows * width)
    scale, shift = spread * gain[:, 0:1], gain[:, 1:2]
    top = jnp.where(tile == 0, 0.0, 1.0)
    bottom = jnp.where(tile == last, 0.0, 1.0)
    for r in range(2):
        put(stack, 0, r, above[2 + r])
        put(stack, 0, rows + 2 + r, below[2 + r])
        put(stack, 1, r, silu_norm(above[r], centre, scale, shift) * top)
        put(stack, 1, rows + 2 + r, silu_norm(below[r], centre, scale, shift) * bottom)
    for r in range(rows):
        put(stack, 0, 2 + r, cache_t[r])
        put(stack, 1, 2 + r, silu_norm(lat_t[r], centre, scale, shift))
    step = 3 * channels
    for r in range(rows + 2):
        acc[r] = dot(weights[0], stack[0, r * step : (r + 3) * step]) + dot(
            weights[2], stack[1, r * step : (r + 3) * step]
        )


def conv_coarse_b(other, above, below, stats, gain, weights, acc, out, stack):
    frame = lax.axis_index("tm")
    tile = lax.axis_index("tile")
    last = lax.axis_size("tile") - 1
    rows, channels, width = other.shape

    @pl.when(frame == 0)
    def _():
        for r in range(2):
            put(stack, 0, r, above[r])
            put(stack, 0, rows + 2 + r, below[r])
        for r in range(rows):
            put(stack, 0, 2 + r, other[r])

    @pl.when(frame != 0)
    def _():
        centre, spread = combine(stats[...], channels, rows * width)
        scale, shift = spread * gain[:, 0:1], gain[:, 1:2]
        top = jnp.where(tile == 0, 0.0, 1.0)
        bottom = jnp.where(tile == last, 0.0, 1.0)
        for r in range(2):
            put(stack, 0, r, silu_norm(above[r], centre, scale, shift) * top)
            put(stack, 0, rows + 2 + r, silu_norm(below[r], centre, scale, shift) * bottom)
        for r in range(rows):
            put(stack, 0, 2 + r, silu_norm(other[r], centre, scale, shift))

    step = 3 * channels
    for r in range(rows + 2):
        value = acc[r] + dot(weights[1], stack[0, r * step : (r + 3) * step])
        if r == 0:
            value = value * jnp.where(tile == 0, 0.0, 1.0)
        if r == rows + 1:
            value = value * jnp.where(tile == last, 0.0, 1.0)
        out[r] = value.astype(bf16)


def raise_rows(coarse, weights, raised, stack):
    rows, channels, width = coarse.shape
    row = lax.broadcasted_iota(jnp.int32, (width, 2 * width), 0)
    col = lax.broadcasted_iota(jnp.int32, (width, 2 * width), 1) // 2
    spread_out = (row == col).astype(f32).astype(bf16)
    for r in range(rows):
        put(stack, 0, r, dot(coarse[r], spread_out))
    step = 3 * channels
    c2 = weights.shape[0] // 2
    for m in range(rows - 1):
        both = dot(weights[...], stack[0, m * step : (m + 2) * step]).astype(bf16)
        raised[2 * m] = both[:c2]
        raised[2 * m + 1] = both[c2:]


def up_kernel(coarse, weights, raised, pay, stack):
    raise_rows(coarse, weights, raised, stack)
    count = raised.shape[0] - 2
    payload(pay, *moments([raised[r + 1] for r in range(count)], count * raised.shape[2]))


def put_active(stack, slot, raised, stats, gain):
    tile = lax.axis_index("tile")
    last = lax.axis_size("tile") - 1
    rows, channels, width = raised.shape
    centre, spread = combine(stats[...], channels, (rows - 2) * width)
    scale, shift = spread * gain[:, 0:1], gain[:, 1:2]
    for r in range(rows):
        value = silu_norm(raised[r], centre, scale, shift)
        if r == 0:
            value = value * jnp.where(tile == 0, 0.0, 1.0)
        if r == rows - 1:
            value = value * jnp.where(tile == last, 0.0, 1.0)
        put(stack, slot, r, value)


def put_cache(stack, slot, fine_t, above, below):
    rows, channels, width = fine_t.shape
    for r, ref in ((0, above), (rows + 1, below)):
        put(stack, slot, r, jnp.concatenate([ref[:channels], ref[channels:]], axis=1))
    for r in range(rows):
        put(stack, slot, r + 1, fine_t[r])


def conv_fine_a(raised, fine_t, above, below, stats, gain, weights, acc, stack):
    put_cache(stack, 0, fine_t, above[4], below[4])
    put_active(stack, 1, raised, stats, gain)
    step = 3 * fine_t.shape[1]
    for m in range(acc.shape[0]):
        window = slice(2 * m * step, (2 * m + 4) * step)
        acc[m] = dot(weights[0], stack[0, window]) + dot(weights[2], stack[1, window])


def conv_fine_b(
    fine_r, edges, coarse_r, stats, gain, weights_up, weights, acc, out, raised, stack_up, stack, rows_out
):
    frame = lax.axis_index("tm")

    @pl.when(frame == 0)
    def _():
        put_cache(stack, 0, fine_r, edges[0], edges[1])

    @pl.when(frame != 0)
    def _():
        raise_rows(coarse_r, weights_up, raised, stack_up)
        put_active(stack, 0, raised, stats, gain)

    c2 = fine_r.shape[1]
    step = 3 * c2
    bias = gain[:, 2:3]
    for m in range(acc.shape[0]):
        window = slice(2 * m * step, (2 * m + 4) * step)
        both = acc[m] + dot(weights[1], stack[0, window])
        rows_out[2 * m] = (both[:c2] + bias).astype(bf16)
        rows_out[2 * m + 1] = (both[c2:] + bias).astype(bf16)
    out[...] = jnp.swapaxes(rows_out[...], 0, 1)


def per_device(
    latent,
    coarse_cache,
    fine_cache,
    gain_coarse,
    shift_coarse,
    weight_coarse,
    weight_up,
    gain_fine,
    shift_fine,
    weight_fine,
    bias_fine,
):
    _, c1, rows, cols = latent.shape
    c2 = fine_cache.shape[1]
    tiles = lax.axis_size("tile")
    fine_rows, fine_cols = 2 * rows, 2 * cols
    forward = [(i, i + 1) for i in range(tiles - 1)]
    backward = [(i + 1, i) for i in range(tiles - 1)]
    later, earlier = [(0, 1)], [(1, 0)]

    def shared(stats):
        return lax.all_to_all(stats, "tile", 0, 0)

    lat_t, cache_t, fine_t, send, pack_up, pack_down, pay = call(
        first_kernel,
        "first",
        [
            ((rows, c1, cols), bf16),
            ((rows, c1, cols), bf16),
            ((fine_rows, c2, fine_cols), bf16),
            ((rows, c1, cols), bf16),
            ((5, c1, cols), bf16),
            ((5, c1, cols), bf16),
            ((tiles, 512), f32),
        ],
    )(latent[0], coarse_cache[0], fine_cache[0])
    above = lax.ppermute(pack_up, "tile", forward)
    below = lax.ppermute(pack_down, "tile", backward)
    other = lax.ppermute(send, "tm", [(0, 1), (1, 0)])
    fine_r = lax.ppermute(fine_t, "tm", earlier)
    w_coarse, w_up, w_fine = call(
        weights_kernel,
        "weights",
        [((3, c1, 9 * c1), bf16), ((2 * c2, 6 * c1), bf16), ((3, 2 * c2, 12 * c2), bf16)],
    )(weight_coarse, weight_up, weight_fine)
    par_coarse = jnp.stack([gain_coarse, shift_coarse], axis=1)
    par_fine = jnp.stack([gain_fine, shift_fine, bias_fine], axis=1)
    edges = lax.ppermute(jnp.stack([above[4], below[4]]), "tm", earlier)

    stats = shared(pay)
    stats_r = lax.ppermute(stats, "tm", later)
    other_above = lax.ppermute(other[rows - 2 :], "tile", forward)
    other_below = lax.ppermute(other[:2], "tile", backward)
    (acc,) = call(
        conv_coarse_a,
        "coarse_a",
        [((rows + 2, c1, cols), f32)],
        [pltpu.VMEM((2, (rows + 4) * 3 * c1, cols), bf16)],
    )(lat_t, cache_t, above, below, stats, par_coarse, w_coarse)
    (coarse,) = call(
        conv_coarse_b,
        "coarse_b",
        [((rows + 2, c1, cols), bf16)],
        [pltpu.VMEM((1, (rows + 4) * 3 * c1, cols), bf16)],
    )(other, other_above, other_below, stats_r, par_coarse, w_coarse, acc)
    coarse_r = lax.ppermute(coarse, "tm", later)
    up_stack = pltpu.VMEM((1, (rows + 2) * 3 * c1, fine_cols), bf16)
    raised, pay = call(
        up_kernel,
        "up",
        [((fine_rows + 2, c2, fine_cols), bf16), ((tiles, 256), f32)],
        [up_stack],
    )(coarse, w_up)
    stats = shared(pay)
    stats_r = lax.ppermute(stats, "tm", later)
    (acc,) = call(
        conv_fine_a,
        "fine_a",
        [((rows, 2 * c2, fine_cols), f32)],
        [pltpu.VMEM((2, (fine_rows + 2) * 3 * c2, fine_cols), bf16)],
    )(raised, fine_t, above, below, stats, par_fine, w_fine)
    (out,) = call(
        conv_fine_b,
        "fine_b",
        [((c2, fine_rows, fine_cols), bf16)],
        [
            pltpu.VMEM((fine_rows + 2, c2, fine_cols), bf16),
            up_stack,
            pltpu.VMEM((1, (fine_rows + 2) * 3 * c2, fine_cols), bf16),
            pltpu.VMEM((fine_rows, c2, fine_cols), bf16),
        ],
    )(fine_r, edges, coarse_r, stats_r, par_fine, w_up, w_fine, acc)
    return out[None]


def solution(mesh):
    split = P("tm", None, "tile", None)
    return jax.shard_map(
        per_device,
        mesh=mesh,
        in_specs=(split,) * 3 + (P(),) * 8,
        out_specs=split,
        check_vma=False,
    )
```

```python
import jax
import jax.numpy as jnp
from jax import lax
from jax.experimental import pallas as pl
from jax.experimental.pallas import tpu as pltpu
from jax.sharding import PartitionSpec as P

GROUPS = 32
EPS = 1e-05
f32 = jnp.float32
bf16 = jnp.bfloat16


def call(kernel, name, outs, scratch=(), local=True, limit=12):
    run = pl.pallas_call(
        kernel,
        out_shape=[pltpu.VMEM(s, d) if local else jax.ShapeDtypeStruct(s, d) for s, d in outs],
        scratch_shapes=list(scratch),
        compiler_params=pltpu.CompilerParams(vmem_limit_bytes=limit * 2**20),
        name=name,
    )

    def with_arrays(*arrays):
        return run(*[pltpu.with_memory_space_constraint(a, pltpu.VMEM) for a in arrays])

    return with_arrays


def dot(a, b):
    return jnp.dot(a, b, preferred_element_type=f32)


def exact(a, b):
    return jnp.dot(a, b, preferred_element_type=f32, precision=lax.Precision.HIGHEST)


def members(channels, transposed=False):
    shape, dim = ((channels, GROUPS), 1) if transposed else ((GROUPS, channels), 0)
    group = lax.broadcasted_iota(jnp.int32, shape, dim)
    channel = lax.broadcasted_iota(jnp.int32, shape, 1 - dim)
    return (group == channel // (channels // GROUPS)).astype(f32)


def moments(rows, count):
    channels = rows[0].shape[0]
    total = rows[0].astype(f32)
    for row in rows[1:]:
        total = total + row.astype(f32)
    total = jnp.broadcast_to(jnp.sum(total, axis=1, keepdims=True), (channels, 128))
    mean = exact(members(channels), total) / (count * (channels // GROUPS))
    centre = exact(members(channels, True), mean)[:, :1]
    squares = None
    for row in rows:
        centred = row.astype(f32) - centre
        squares = centred * centred if squares is None else squares + centred * centred
    squares = jnp.broadcast_to(jnp.sum(squares, axis=1, keepdims=True), (channels, 128))
    return mean, exact(members(channels), squares)


def payload(ref, mean, squares):
    both = jnp.concatenate([mean, squares, mean, squares], axis=0)
    ref[...] = jnp.broadcast_to(jnp.transpose(both)[0:1][None], ref.shape)


def column(ref):
    return jnp.transpose(jnp.broadcast_to(ref[...], (128, ref.shape[1])))[:, :1]


def combine(stats, frame, channels, per_device):
    devices = lax.axis_size("tile")
    turned = jnp.transpose(stats[pl.ds(frame * devices, devices)].reshape(devices, 4 * GROUPS))
    mean, squares = turned[:GROUPS], turned[GROUPS : 2 * GROUPS]
    size = per_device * (channels // GROUPS)
    centre = jnp.sum(mean, axis=1, keepdims=True) / devices
    away = mean - centre
    total = jnp.sum(squares + size * (away * away), axis=1, keepdims=True)
    spread = lax.rsqrt(total / (devices * size) + EPS)
    lane = lax.broadcasted_iota(jnp.int32, (GROUPS, 128), 1)
    wide = exact(members(channels, True), jnp.where(lane == 0, centre, spread))
    return wide[:, 0:1], wide[:, 1:2]


def silu_norm(x, centre, scale, shift):
    half = 0.5 * ((x[...].astype(f32) - centre) * scale + shift)
    return half + half * jnp.tanh(half)


def put(ref, slot, row, x):
    channels, width = x.shape
    lane = lax.broadcasted_iota(jnp.int32, (channels, width), 1)
    wide = x.astype(f32)
    left = jnp.where(lane == 0, 0.0, pltpu.roll(wide, 1, 1))
    right = jnp.where(lane == width - 1, 0.0, pltpu.roll(wide, width - 1, 1))
    base = row * 3 * channels
    ref[slot, base : base + channels] = left.astype(bf16)
    ref[slot, base + channels : base + 2 * channels] = x.astype(bf16)
    ref[slot, base + 2 * channels : base + 3 * channels] = right.astype(bf16)


def weights_kernel(coarse, up, fine, out_coarse, out_up, out_fine):
    c1, c2 = coarse.shape[3], fine.shape[3]
    for t in range(3):
        for a in range(3):
            for b in range(3):
                at = (a * 3 + b) * c1
                out_coarse[t, :, at : at + c1] = coarse[t, a, b]
    for b in range(3):
        first, second, third = (up[a, b].astype(f32) for a in range(3))
        at = b * c1
        for rows, a, value in (
            (0, 0, first + second),
            (0, 1, third),
            (1, 0, first),
            (1, 1, second + third),
        ):
            out_up[rows * c2 : (rows + 1) * c2, a * 3 * c1 + at : a * 3 * c1 + at + c1] = (
                value.astype(bf16)
            )
    out_fine[...] = jnp.zeros(out_fine.shape, bf16)
    for t in range(3):
        for a in range(3):
            for b in range(3):
                block = fine[t, a, b]
                for rho in range(2):
                    at = ((a + rho) * 3 + b) * c2
                    out_fine[t, rho * c2 : (rho + 1) * c2, at : at + c2] = block


def turn_kernel(latent, cache, fine, lat_t, cache_t, send, up, down):
    rows, width = latent.shape[1:]
    c2 = fine.shape[0]
    lat_t[...] = jnp.swapaxes(latent[...], 0, 1)
    cache_t[...] = jnp.swapaxes(cache[...], 0, 1)
    for ref, cut, line in (
        (up, slice(rows - 2, rows), fine[:, 2 * rows - 1, :]),
        (down, slice(0, 2), fine[:, 0, :]),
    ):
        ref[0:2] = lat_t[cut]
        ref[2:4] = cache_t[cut]
        ref[4, :c2] = line[:, :width]
        ref[4, c2:] = line[:, width:]

    @pl.when(lax.axis_index("tm") == 0)
    def _():
        send[...] = lat_t[...]

    @pl.when(lax.axis_index("tm") != 0)
    def _():
        send[...] = cache_t[...]


def moments_kernel(lat_t, fine, pay, fine_t):
    rows, _, width = lat_t.shape
    fine_t[...] = jnp.swapaxes(fine[...], 0, 1)
    payload(pay, *moments([lat_t[r] for r in range(rows)], rows * width))


def coarse_first(cache_t, above, below, fine_t, weights, acc, fine_pad, stack):
    rows, channels, width = cache_t.shape
    fine_rows, c2, _ = fine_t.shape
    fine_pad[1 : fine_rows + 1] = fine_t[...]
    for r, ref in ((0, above), (fine_rows + 1, below)):
        fine_pad[r, :, :width] = ref[4, :c2]
        fine_pad[r, :, width:] = ref[4, c2:]
    for r in range(2):
        put(stack, 0, r, above[2 + r])
        put(stack, 0, rows + 2 + r, below[2 + r])
    for r in range(rows):
        put(stack, 0, 2 + r, cache_t[r])
    step = 3 * channels
    for r in range(rows + 2):
        acc[r] = dot(weights[0], stack[0, r * step : (r + 3) * step])


def put_normed(stack, middle, above, below, stats, frame, gain, shift):
    tile = lax.axis_index("tile")
    last = lax.axis_size("tile") - 1
    rows, (channels, width) = len(middle), middle[0].shape
    centre, spread = combine(stats, frame, channels, rows * width)
    scale, offset = spread * column(gain), column(shift)
    top = jnp.where(tile == 0, 0.0, 1.0)
    bottom = jnp.where(tile == last, 0.0, 1.0)
    for r in range(2):
        put(stack, 0, r, silu_norm(above[r], centre, scale, offset) * top)
        put(stack, 0, rows + 2 + r, silu_norm(below[r], centre, scale, offset) * bottom)
    for r in range(rows):
        put(stack, 0, 2 + r, silu_norm(middle[r], centre, scale, offset))


def rows_of(*refs):
    return [ref.at[r] for ref in refs for r in range(ref.shape[0])]


def coarse_third(lat_t, above, below, stats, gain, shift, weights, acc, out, stack):
    frame = lax.axis_index("tm")
    put_normed(
        stack, rows_of(lat_t), rows_of(above), rows_of(below), stats, frame, gain, shift
    )
    rows, channels, _ = lat_t.shape
    step = 3 * channels
    for r in range(rows + 2):
        out[r] = acc[r] + dot(weights[2], stack[0, r * step : (r + 3) * step])


def coarse_second(
    other, above, below, stats, gain, shift, weights, acc, out, stack
):
    frame = lax.axis_index("tm")
    tile = lax.axis_index("tile")
    last = lax.axis_size("tile") - 1
    rows, channels, _ = other.shape
    other, above, below = rows_of(other), rows_of(above), rows_of(below)

    @pl.when(frame == 0)
    def _():
        for r, ref in enumerate(above + other + below):
            put(stack, 0, r, ref[...])

    @pl.when(frame != 0)
    def _():
        put_normed(stack, other, above, below, stats, 0, gain, shift)

    step = 3 * channels
    for r in range(rows + 2):
        value = acc[r] + dot(weights[1], stack[0, r * step : (r + 3) * step])
        if r == 0:
            value = value * jnp.where(tile == 0, 0.0, 1.0)
        if r == rows + 1:
            value = value * jnp.where(tile == last, 0.0, 1.0)
        out[r] = value.astype(bf16)


def raise_rows(coarse, weights, raised, stack):
    rows, (channels, width) = len(coarse), coarse[0].shape
    row = lax.broadcasted_iota(jnp.int32, (width, 2 * width), 0)
    col = lax.broadcasted_iota(jnp.int32, (width, 2 * width), 1) // 2
    spread_out = (row == col).astype(f32).astype(bf16)
    for r in range(rows):
        put(stack, 0, r, dot(coarse[r][...], spread_out))
    step = 3 * channels
    c2 = weights.shape[0] // 2
    for m in range(rows - 1):
        both = dot(weights[...], stack[0, m * step : (m + 2) * step]).astype(bf16)
        raised[2 * m] = both[:c2]
        raised[2 * m + 1] = both[c2:]


def up_kernel(coarse, weights, raised, pay, stack):
    raise_rows(rows_of(coarse), weights, raised, stack)
    count = raised.shape[0] - 2
    payload(pay, *moments([raised[r + 1] for r in range(count)], count * raised.shape[2]))


def put_active(stack, raised, stats, frame, gain, shift):
    tile = lax.axis_index("tile")
    last = lax.axis_size("tile") - 1
    rows, channels, width = raised.shape
    centre, spread = combine(stats, frame, channels, (rows - 2) * width)
    scale, offset = spread * column(gain), column(shift)
    for r in range(rows):
        value = silu_norm(raised[r], centre, scale, offset)
        if r == 0:
            value = value * jnp.where(tile == 0, 0.0, 1.0)
        if r == rows - 1:
            value = value * jnp.where(tile == last, 0.0, 1.0)
        put(stack, 0, r, value)


def put_cache(stack, fine):
    for r in range(fine.shape[0]):
        put(stack, 0, r, fine[r])


def fine_window(stack, m, step):
    return stack[0, 2 * m * step : (2 * m + 4) * step]


def fine_first(fine, weights, acc, stack):
    put_cache(stack, fine)
    for m in range(acc.shape[0]):
        acc[m] = dot(weights[0], fine_window(stack, m, 3 * fine.shape[1]))


def fine_third(raised, stats, gain, shift, weights, acc, out, stack):
    put_active(stack, raised, stats, lax.axis_index("tm"), gain, shift)
    for m in range(acc.shape[0]):
        out[m] = acc[m] + dot(weights[2], fine_window(stack, m, 3 * raised.shape[1]))


def fine_second(
    fine, coarse, stats, gain, shift, bias, weights_up, weights, acc, out,
    raised, stack_up, stack, turned,
):
    frame = lax.axis_index("tm")

    @pl.when(frame == 0)
    def _():
        put_cache(stack, fine)

    @pl.when(frame != 0)
    def _():
        raise_rows(rows_of(coarse), weights_up, raised, stack_up)
        put_active(stack, raised, stats, 0, gain, shift)

    c2 = fine.shape[1]
    offset = column(bias)
    for m in range(acc.shape[0]):
        both = acc[m] + dot(weights[1], fine_window(stack, m, 3 * c2))
        turned[2 * m] = (both[:c2] + offset).astype(bf16)
        turned[2 * m + 1] = (both[c2:] + offset).astype(bf16)
    out[...] = jnp.swapaxes(turned[...], 0, 1)


def per_device(
    latent,
    coarse_cache,
    fine_cache,
    gain_coarse,
    shift_coarse,
    weight_coarse,
    weight_up,
    gain_fine,
    shift_fine,
    weight_fine,
    bias_fine,
):
    _, c1, rows, cols = latent.shape
    c2 = fine_cache.shape[1]
    tiles = lax.axis_size("tile")
    fine_rows, fine_cols = 2 * rows, 2 * cols
    forward = [(i, i + 1) for i in range(tiles - 1)]
    backward = [(i + 1, i) for i in range(tiles - 1)]
    later, earlier = [(0, 1)], [(1, 0)]
    gain_coarse, shift_coarse = gain_coarse[None], shift_coarse[None]
    gain_fine, shift_fine, bias_fine = gain_fine[None], shift_fine[None], bias_fine[None]

    def shared(stats):
        return lax.all_to_all(stats, ("tm", "tile"), 0, 0)

    def after(value, *others):
        return lax.optimization_barrier((value, *others))[0]

    devices = lax.axis_size("tm") * tiles
    coarse_shape, coarse_acc = (rows, c1, cols), ((rows + 2, c1, cols), f32)
    fine_acc = ((rows, 2 * c2, fine_cols), f32)
    coarse_stack = pltpu.VMEM((1, (rows + 4) * 3 * c1, cols), bf16)
    fine_stack = pltpu.VMEM((1, (fine_rows + 2) * 3 * c2, fine_cols), bf16)
    up_stack = pltpu.VMEM((1, (rows + 2) * 3 * c1, fine_cols), bf16)
    raised_shape = ((fine_rows + 2, c2, fine_cols), bf16)

    rim = ((5, c1, cols), bf16)
    lat_t, cache_t, send, rim_up, rim_down = call(
        turn_kernel, "turn", [(coarse_shape, bf16)] * 3 + [rim] * 2
    )(latent[0], coarse_cache[0], fine_cache[0])
    above = lax.ppermute(rim_up, "tile", forward)
    below = lax.ppermute(rim_down, "tile", backward)
    other = lax.ppermute(send, "tm", [(0, 1), (1, 0)])
    pay, fine_t = call(
        moments_kernel, "moments", [((devices, 1, 4 * GROUPS), f32), ((fine_rows, c2, fine_cols), bf16)]
    )(lat_t, fine_cache[0])
    w_coarse, w_up, w_fine = call(
        weights_kernel,
        "weights",
        [((3, c1, 9 * c1), bf16), ((2 * c2, 6 * c1), bf16), ((3, 2 * c2, 12 * c2), bf16)],
    )(weight_coarse, weight_up, weight_fine)
    stats = shared(after(pay, w_coarse, above, below))
    acc, fine_pad = call(
        coarse_first, "coarse_first", [coarse_acc, raised_shape], [coarse_stack]
    )(after(cache_t, stats), above, below, fine_t, w_coarse)
    other = after(other, stats)
    other_above = lax.ppermute(other[rows - 2 :], "tile", forward)
    other_below = lax.ppermute(other[:2], "tile", backward)
    (acc,) = call(coarse_third, "coarse_third", [coarse_acc], [coarse_stack])(
        lat_t,
        above,
        below,
        stats,
        gain_coarse,
        shift_coarse,
        w_coarse,
        after(acc, other_above, other_below),
    )
    fine_r = lax.ppermute(after(fine_pad, other_above, other_below), "tm", earlier)
    (coarse,) = call(
        coarse_second, "coarse_second", [((rows + 2, c1, cols), bf16)], [coarse_stack]
    )(other, other_above, other_below, stats, gain_coarse, shift_coarse, w_coarse, acc)
    coarse_r = lax.ppermute(coarse, "tm", later)
    raised, pay = call(up_kernel, "up", [raised_shape, ((devices, 1, 4 * GROUPS), f32)], [up_stack])(
        coarse, w_up
    )
    (acc,) = call(fine_first, "fine_first", [fine_acc], [fine_stack])(fine_pad, w_fine)

    stats = shared(after(pay, acc))
    (acc,) = call(fine_third, "fine_third", [fine_acc], [fine_stack])(
        raised, stats, gain_fine, shift_fine, w_fine, acc
    )
    (out,) = call(
        fine_second,
        "fine_second",
        [((c2, fine_rows, fine_cols), bf16)],
        [
            pltpu.VMEM(*raised_shape),
            up_stack,
            fine_stack,
            pltpu.VMEM((fine_rows, c2, fine_cols), bf16),
        ],
        local=False,
        limit=20,
    )(
        fine_r, coarse_r, stats, gain_fine, shift_fine, bias_fine, w_up, w_fine, acc
    )
    return out[None]


def solution(mesh):
    split = P("tm", None, "tile", None)
    return jax.shard_map(
        per_device,
        mesh=mesh,
        in_specs=(split,) * 3 + (P(),) * 8,
        out_specs=split,
        check_vma=False,
    )
```

```python
import jax
import jax.numpy as jnp
from jax import lax
from jax.experimental import pallas as pl
from jax.experimental.pallas import tpu as pltpu
from jax.sharding import PartitionSpec as P

GROUPS = 32
EPS = 1e-05
f32 = jnp.float32
bf16 = jnp.bfloat16


def call(kernel, name, outs, scratch=(), local=True, limit=12, far=0, aliases=None):
    def with_arrays(*arrays):
        near = [pltpu.with_memory_space_constraint(a, pltpu.VMEM) for a in arrays[far:]]
        away = [pltpu.with_memory_space_constraint(a, pltpu.HBM) for a in arrays[:far]]
        return pl.pallas_call(
            kernel,
            in_specs=[pl.BlockSpec(memory_space=pltpu.HBM)] * far
            + [pl.BlockSpec(memory_space=pltpu.VMEM)] * len(near),
            out_shape=[pltpu.VMEM(s, d) if local else jax.ShapeDtypeStruct(s, d) for s, d in outs],
            scratch_shapes=list(scratch),
            input_output_aliases=aliases or {},
            compiler_params=pltpu.CompilerParams(vmem_limit_bytes=limit * 2**20),
            name=name,
        )(*away, *near)

    return with_arrays


def dot(a, b):
    return jnp.dot(a, b, preferred_element_type=f32)


def exact(a, b):
    return jnp.dot(a, b, preferred_element_type=f32, precision=lax.Precision.HIGHEST)


def members(channels, transposed=False):
    shape, dim = ((channels, GROUPS), 1) if transposed else ((GROUPS, channels), 0)
    group = lax.broadcasted_iota(jnp.int32, shape, dim)
    channel = lax.broadcasted_iota(jnp.int32, shape, 1 - dim)
    return (group == channel // (channels // GROUPS)).astype(f32)


def moments(rows, count):
    channels = rows[0].shape[0]
    total = rows[0].astype(f32)
    for row in rows[1:]:
        total = total + row.astype(f32)
    total = jnp.broadcast_to(jnp.sum(total, axis=1, keepdims=True), (channels, 128))
    mean = exact(members(channels), total) / (count * (channels // GROUPS))
    centre = exact(members(channels, True), mean)[:, :1]
    squares = None
    for row in rows:
        centred = row.astype(f32) - centre
        squares = centred * centred if squares is None else squares + centred * centred
    squares = jnp.broadcast_to(jnp.sum(squares, axis=1, keepdims=True), (channels, 128))
    return mean, exact(members(channels), squares)


def payload(ref, mean, squares):
    both = jnp.concatenate([mean, squares, mean, squares], axis=0)
    ref[...] = jnp.broadcast_to(jnp.transpose(both)[0:1][None], ref.shape)


def column(ref):
    return jnp.transpose(jnp.broadcast_to(ref[...], (128, ref.shape[1])))[:, :1]


def combine(stats, frame, channels, per_device):
    devices = lax.axis_size("tile")
    turned = jnp.transpose(stats[pl.ds(frame * devices, devices)].reshape(devices, 4 * GROUPS))
    mean, squares = turned[:GROUPS], turned[GROUPS : 2 * GROUPS]
    size = per_device * (channels // GROUPS)
    centre = jnp.sum(mean, axis=1, keepdims=True) / devices
    away = mean - centre
    total = jnp.sum(squares + size * (away * away), axis=1, keepdims=True)
    spread = lax.rsqrt(total / (devices * size) + EPS)
    lane = lax.broadcasted_iota(jnp.int32, (GROUPS, 128), 1)
    wide = exact(members(channels, True), jnp.where(lane == 0, centre, spread))
    return wide[:, 0:1], wide[:, 1:2]


def silu_norm(x, centre, scale, shift):
    half = 0.5 * ((x[...].astype(f32) - centre) * scale + shift)
    return half + half * jnp.tanh(half)


def put(ref, slot, row, x):
    channels, width = x.shape
    lane = lax.broadcasted_iota(jnp.int32, (channels, width), 1)
    x = x.astype(bf16)
    none = jnp.zeros((), bf16)
    left = jnp.where(lane == 0, none, pltpu.roll(x, 1, 1))
    right = jnp.where(lane == width - 1, none, pltpu.roll(x, width - 1, 1))
    base = row * 3 * channels
    ref[slot, base : base + channels] = left
    ref[slot, base + channels : base + 2 * channels] = x
    ref[slot, base + 2 * channels : base + 3 * channels] = right


def weights_kernel(coarse, up, fine, out_coarse, out_up, out_fine):
    c1, c2 = coarse.shape[3], fine.shape[3]
    for t in range(3):
        for a in range(3):
            for b in range(3):
                at = (a * 3 + b) * c1
                out_coarse[t, :, at : at + c1] = coarse[t, a, b]
    for b in range(3):
        first, second, third = (up[a, b].astype(f32) for a in range(3))
        at = b * c1
        for rows, a, value in (
            (0, 0, first + second),
            (0, 1, third),
            (1, 0, first),
            (1, 1, second + third),
        ):
            out_up[rows * c2 : (rows + 1) * c2, a * 3 * c1 + at : a * 3 * c1 + at + c1] = (
                value.astype(bf16)
            )
    out_fine[...] = jnp.zeros(out_fine.shape, bf16)
    for t in range(3):
        for a in range(3):
            for b in range(3):
                block = fine[t, a, b]
                for rho in range(2):
                    at = ((a + rho) * 3 + b) * c2
                    out_fine[t, rho * c2 : (rho + 1) * c2, at : at + c2] = block


CHUNKS = 4


def fetches(source, target, arrived):
    part = source.shape[0] // CHUNKS
    cuts = [pl.ds(k * part, part) for k in range(CHUNKS)]
    return [
        pltpu.make_async_copy(source.at[cut], target.at[cut], arrived.at[k])
        for k, cut in enumerate(cuts)
    ]


def turn_kernel(
    latent, cache, fine, lat_t, cache_t, send, fine_v, lat_v, cache_v, lat_in, cache_in, fine_in
):
    lat_copies = fetches(latent, lat_v, lat_in)
    cache_copies = fetches(cache, cache_v, cache_in)
    fine_copies = fetches(fine, fine_v, fine_in)
    for copy in lat_copies + cache_copies + fine_copies:
        copy.start()
    for copy in lat_copies:
        copy.wait()
    lat_t[...] = jnp.swapaxes(lat_v[...], 0, 1)
    for copy in cache_copies:
        copy.wait()
    cache_t[...] = jnp.swapaxes(cache_v[...], 0, 1)

    @pl.when(lax.axis_index("tm") == 0)
    def _():
        send[...] = lat_t[...]

    @pl.when(lax.axis_index("tm") != 0)
    def _():
        send[...] = cache_t[...]

    for copy in fine_copies:
        copy.wait()


def moments_kernel(lat_t, cache_t, fine, pay, fine_t, up, down):
    rows, _, width = lat_t.shape
    c2 = fine.shape[0]
    fine_t[...] = jnp.swapaxes(fine[...], 0, 1)
    for ref, cut, line in (
        (up, slice(rows - 2, rows), fine_t[2 * rows - 1]),
        (down, slice(0, 2), fine_t[0]),
    ):
        ref[0:2] = lat_t[cut]
        ref[2:4] = cache_t[cut]
        ref[4, :c2] = line[:, :width]
        ref[4, c2:] = line[:, width:]
    payload(pay, *moments([lat_t[r] for r in range(rows)], rows * width))


def coarse_first(cache_t, above, below, fine_t, weights, acc, fine_a, fine_b, stack):
    rows, channels, width = cache_t.shape
    c2 = fine_t.shape[1]
    early, late = fine_a.shape[0], fine_b.shape[0]
    fine_a[1:] = fine_t[: early - 1]
    fine_b[: late - 1] = fine_t[early - 1 :]
    for rim, ref in ((fine_a.at[0], above), (fine_b.at[late - 1], below)):
        rim[:, :width] = ref[4, :c2]
        rim[:, width:] = ref[4, c2:]
    for r in range(2):
        put(stack, 0, r, above[2 + r])
        put(stack, 0, rows + 2 + r, below[2 + r])
    for r in range(rows):
        put(stack, 0, 2 + r, cache_t[r])
    step = 3 * channels
    for r in range(rows + 2):
        acc[r] = dot(weights[0], stack[0, r * step : (r + 3) * step])


def put_normed(stack, middle, above, below, stats, frame, gain, shift):
    tile = lax.axis_index("tile")
    last = lax.axis_size("tile") - 1
    rows, (channels, width) = len(middle), middle[0].shape
    centre, spread = combine(stats, frame, channels, rows * width)
    scale, offset = spread * column(gain), column(shift)
    top = jnp.where(tile == 0, 0.0, 1.0)
    bottom = jnp.where(tile == last, 0.0, 1.0)
    for r in range(2):
        put(stack, 0, r, silu_norm(above[r], centre, scale, offset) * top)
        put(stack, 0, rows + 2 + r, silu_norm(below[r], centre, scale, offset) * bottom)
    for r in range(rows):
        put(stack, 0, 2 + r, silu_norm(middle[r], centre, scale, offset))


def rows_of(*refs):
    return [ref.at[r] for ref in refs for r in range(ref.shape[0])]


def coarse_third(lat_t, above, below, stats, gain, shift, weights, acc, out, stack):
    frame = lax.axis_index("tm")
    put_normed(
        stack, rows_of(lat_t), rows_of(above), rows_of(below), stats, frame, gain, shift
    )
    rows, channels, _ = lat_t.shape
    step = 3 * channels
    for r in range(rows + 2):
        out[r] = acc[r] + dot(weights[2], stack[0, r * step : (r + 3) * step])


def coarse_second(
    other, above, below, stats, gain, shift, weights, acc, out, stack
):
    frame = lax.axis_index("tm")
    tile = lax.axis_index("tile")
    last = lax.axis_size("tile") - 1
    rows, channels, _ = other.shape
    other, above, below = rows_of(other), rows_of(above), rows_of(below)

    @pl.when(frame == 0)
    def _():
        for r, ref in enumerate(above + other + below):
            put(stack, 0, r, ref[...])

    @pl.when(frame != 0)
    def _():
        put_normed(stack, other, above, below, stats, 0, gain, shift)

    step = 3 * channels
    for r in range(rows + 2):
        value = acc[r] + dot(weights[1], stack[0, r * step : (r + 3) * step])
        if r == 0:
            value = value * jnp.where(tile == 0, 0.0, 1.0)
        if r == rows + 1:
            value = value * jnp.where(tile == last, 0.0, 1.0)
        out[r] = value.astype(bf16)


def raise_rows(coarse, weights, raised, stack):
    rows, (channels, width) = len(coarse), coarse[0].shape
    row = lax.broadcasted_iota(jnp.int32, (width, 2 * width), 0)
    col = lax.broadcasted_iota(jnp.int32, (width, 2 * width), 1) // 2
    spread_out = (row == col).astype(f32).astype(bf16)
    for r in range(rows):
        put(stack, 0, r, dot(coarse[r][...], spread_out))
    step = 3 * channels
    c2 = weights.shape[0] // 2
    for m in range(rows - 1):
        both = dot(weights[...], stack[0, m * step : (m + 2) * step]).astype(bf16)
        raised[2 * m] = both[:c2]
        raised[2 * m + 1] = both[c2:]


def up_kernel(coarse, weights, raised, pay, stack):
    raise_rows(rows_of(coarse), weights, raised, stack)
    count = raised.shape[0] - 2
    payload(pay, *moments([raised[r + 1] for r in range(count)], count * raised.shape[2]))


def put_active(stack, raised, stats, frame, gain, shift):
    tile = lax.axis_index("tile")
    last = lax.axis_size("tile") - 1
    rows, channels, width = raised.shape
    centre, spread = combine(stats, frame, channels, (rows - 2) * width)
    scale, offset = spread * column(gain), column(shift)
    for r in range(rows):
        value = silu_norm(raised[r], centre, scale, offset)
        if r == 0:
            value = value * jnp.where(tile == 0, 0.0, 1.0)
        if r == rows - 1:
            value = value * jnp.where(tile == last, 0.0, 1.0)
        put(stack, 0, r, value)


def put_cache(stack, start, fine):
    for r in range(fine.shape[0]):
        put(stack, 0, start + r, fine[r])


def fine_window(stack, m, step):
    return stack[0, 2 * m * step : (2 * m + 4) * step]


def fine_first(fine_a, fine_b, weights, acc, stack):
    put_cache(stack, 0, fine_a)
    put_cache(stack, fine_a.shape[0], fine_b)
    for m in range(acc.shape[0]):
        acc[m] = dot(weights[0], fine_window(stack, m, 3 * fine_a.shape[1]))


def fine_third(raised, stats, gain, shift, weights, acc, out, stack):
    put_active(stack, raised, stats, lax.axis_index("tm"), gain, shift)
    for m in range(acc.shape[0]):
        out[m] = acc[m] + dot(weights[2], fine_window(stack, m, 3 * raised.shape[1]))


def raise_other(coarse, weights, raised, stack):
    @pl.when(lax.axis_index("tm") != 0)
    def _():
        raise_rows(rows_of(coarse), weights, raised, stack)


def fine_stack(fine_a, raised, stats, gain, shift, stack):
    frame = lax.axis_index("tm")

    @pl.when(frame == 0)
    def _():
        put_cache(stack, 0, fine_a)

    @pl.when(frame != 0)
    def _():
        put_active(stack, raised, stats, 0, gain, shift)


def fine_second(partial, fine_b, bias, weights, acc, out, stack, turned):
    late, c2, _ = fine_b.shape
    start = 2 * acc.shape[0] + 2 - late
    cut = start * 3 * c2

    @pl.when(lax.axis_index("tm") == 0)
    def _():
        put_cache(stack, start, fine_b)

    @pl.when(lax.axis_index("tm") != 0)
    def _():
        stack[0, cut:] = partial[0, cut:]

    offset = column(bias)
    whole = cut // (6 * c2) - 1
    for m in range(acc.shape[0]):
        if m < whole:
            window = fine_window(partial, m, 3 * c2)
        else:
            if m == whole:
                stack[0, 2 * m * 3 * c2 : cut] = partial[0, 2 * m * 3 * c2 : cut]
            window = fine_window(stack, m, 3 * c2)
        both = acc[m] + dot(weights[1], window)
        turned[2 * m] = (both[:c2] + offset).astype(bf16)
        turned[2 * m + 1] = (both[c2:] + offset).astype(bf16)
    out[...] = jnp.swapaxes(turned[...], 0, 1)


def per_device(
    latent,
    coarse_cache,
    fine_cache,
    gain_coarse,
    shift_coarse,
    weight_coarse,
    weight_up,
    gain_fine,
    shift_fine,
    weight_fine,
    bias_fine,
):
    _, c1, rows, cols = latent.shape
    c2 = fine_cache.shape[1]
    tiles = lax.axis_size("tile")
    fine_rows, fine_cols = 2 * rows, 2 * cols
    forward = [(i, i + 1) for i in range(tiles - 1)]
    backward = [(i + 1, i) for i in range(tiles - 1)]
    later, earlier = [(0, 1)], [(1, 0)]
    gain_coarse, shift_coarse = gain_coarse[None], shift_coarse[None]
    gain_fine, shift_fine, bias_fine = gain_fine[None], shift_fine[None], bias_fine[None]

    def shared(stats):
        return lax.all_to_all(stats, ("tm", "tile"), 0, 0)

    def after(value, *others):
        return lax.optimization_barrier((value, *others))[0]

    devices = lax.axis_size("tm") * tiles
    coarse_shape, coarse_acc = (rows, c1, cols), ((rows + 2, c1, cols), f32)
    fine_acc = ((rows, 2 * c2, fine_cols), f32)
    coarse_stack = pltpu.VMEM((1, (rows + 4) * 3 * c1, cols), bf16)
    stack_shape = ((1, (fine_rows + 2) * 3 * c2, fine_cols), bf16)
    fine_scratch = pltpu.VMEM(*stack_shape)
    up_stack = pltpu.VMEM((1, (rows + 2) * 3 * c1, fine_cols), bf16)
    raised_shape = ((fine_rows + 2, c2, fine_cols), bf16)

    rim = ((5, c1, cols), bf16)
    early = fine_rows + 2 - 2
    fine_raw = ((c2, fine_rows, fine_cols), bf16)
    lat_t, cache_t, send, fine_v = call(
        turn_kernel,
        "turn",
        [(coarse_shape, bf16)] * 3 + [fine_raw],
        [pltpu.VMEM((c1, rows, cols), bf16)] * 2 + [pltpu.SemaphoreType.DMA((CHUNKS,))] * 3,
        far=3,
    )(latent[0], coarse_cache[0], fine_cache[0])
    other = lax.ppermute(send, "tm", [(0, 1), (1, 0)])
    pay, fine_t, rim_up, rim_down = call(
        moments_kernel,
        "moments",
        [((devices, 1, 4 * GROUPS), f32), ((fine_rows, c2, fine_cols), bf16)] + [rim] * 2,
    )(lat_t, cache_t, fine_v)
    above = lax.ppermute(rim_up, "tile", forward)
    below = lax.ppermute(rim_down, "tile", backward)
    w_coarse, w_up, w_fine = call(
        weights_kernel,
        "weights",
        [((3, c1, 9 * c1), bf16), ((2 * c2, 6 * c1), bf16), ((3, 2 * c2, 12 * c2), bf16)],
    )(weight_coarse, weight_up, weight_fine)
    stats = shared(after(pay, w_coarse))
    stats, other, above, below = lax.optimization_barrier((stats, other, above, below))
    acc, fine_a, fine_b = call(
        coarse_first,
        "coarse_first",
        [
            coarse_acc,
            ((early, c2, fine_cols), bf16),
            ((fine_rows + 2 - early, c2, fine_cols), bf16),
        ],
        [coarse_stack],
    )(cache_t, above, below, fine_t, w_coarse)
    other_above = lax.ppermute(other[rows - 2 :], "tile", forward)
    other_below = lax.ppermute(other[:2], "tile", backward)
    (acc,) = call(coarse_third, "coarse_third", [coarse_acc], [coarse_stack])(
        lat_t,
        above,
        below,
        stats,
        gain_coarse,
        shift_coarse,
        w_coarse,
        after(acc, other_above, other_below),
    )
    fine_ra = lax.ppermute(after(fine_a, other_above, other_below), "tm", earlier)
    (coarse,) = call(
        coarse_second, "coarse_second", [((rows + 2, c1, cols), bf16)], [coarse_stack]
    )(other, other_above, other_below, stats, gain_coarse, shift_coarse, w_coarse, acc)
    coarse_r = lax.ppermute(coarse, "tm", later)
    raised, pay = call(up_kernel, "up", [raised_shape, ((devices, 1, 4 * GROUPS), f32)], [up_stack])(
        coarse, w_up
    )
    (acc,) = call(fine_first, "fine_first", [fine_acc], [fine_scratch])(fine_a, fine_b, w_fine)

    stats = shared(after(pay, acc))
    stats, fine_ra, coarse_r = lax.optimization_barrier((stats, fine_ra, coarse_r))
    (raised_r,) = call(raise_other, "raise_other", [raised_shape], [up_stack])(coarse_r, w_up)
    fine_rb = lax.ppermute(after(fine_b, raised_r), "tm", earlier)
    (acc,) = call(fine_third, "fine_third", [fine_acc], [fine_scratch])(
        raised, stats, gain_fine, shift_fine, w_fine, acc
    )
    (partial,) = call(fine_stack, "fine_stack", [stack_shape])(
        fine_ra, raised_r, stats, gain_fine, shift_fine
    )
    (out,) = call(
        fine_second,
        "fine_second",
        [fine_raw],
        [fine_scratch, pltpu.VMEM((fine_rows, c2, fine_cols), bf16)],
        local=False,
    )(partial, fine_rb, bias_fine, w_fine, acc)
    return out[None]


def solution(mesh):
    split = P("tm", None, "tile", None)
    return jax.shard_map(
        per_device,
        mesh=mesh,
        in_specs=(split,) * 3 + (P(),) * 8,
        out_specs=split,
        check_vma=False,
    )
```

```python
import jax
import jax.numpy as jnp
from jax import lax
from jax.experimental import pallas as pl
from jax.experimental.pallas import tpu as pltpu
from jax.sharding import PartitionSpec as P

GROUPS = 32
EPS = 1e-05
f32 = jnp.float32
bf16 = jnp.bfloat16


def call(kernel, name, outs, scratch=(), local=True, limit=12, far=0, aliases=None):
    def with_arrays(*arrays):
        near = [pltpu.with_memory_space_constraint(a, pltpu.VMEM) for a in arrays[far:]]
        away = [pltpu.with_memory_space_constraint(a, pltpu.HBM) for a in arrays[:far]]
        return pl.pallas_call(
            kernel,
            in_specs=[pl.BlockSpec(memory_space=pltpu.HBM)] * far
            + [pl.BlockSpec(memory_space=pltpu.VMEM)] * len(near),
            out_shape=[pltpu.VMEM(s, d) if local else jax.ShapeDtypeStruct(s, d) for s, d in outs],
            scratch_shapes=list(scratch),
            input_output_aliases=aliases or {},
            compiler_params=pltpu.CompilerParams(vmem_limit_bytes=limit * 2**20),
            name=name,
        )(*away, *near)

    return with_arrays


def dot(a, b):
    return jnp.dot(a, b, preferred_element_type=f32)


def exact(a, b):
    return jnp.dot(a, b, preferred_element_type=f32, precision=lax.Precision.HIGHEST)


def members(channels, transposed=False):
    shape, dim = ((channels, GROUPS), 1) if transposed else ((GROUPS, channels), 0)
    group = lax.broadcasted_iota(jnp.int32, shape, dim)
    channel = lax.broadcasted_iota(jnp.int32, shape, 1 - dim)
    return (group == channel // (channels // GROUPS)).astype(f32)


def moments(rows, count):
    channels = rows[0].shape[0]
    total = rows[0].astype(f32)
    for row in rows[1:]:
        total = total + row.astype(f32)
    total = jnp.broadcast_to(jnp.sum(total, axis=1, keepdims=True), (channels, 128))
    mean = exact(members(channels), total) / (count * (channels // GROUPS))
    centre = exact(members(channels, True), mean)[:, :1]
    squares = None
    for row in rows:
        centred = row.astype(f32) - centre
        squares = centred * centred if squares is None else squares + centred * centred
    squares = jnp.broadcast_to(jnp.sum(squares, axis=1, keepdims=True), (channels, 128))
    return mean, exact(members(channels), squares)


def payload(ref, mean, squares):
    both = jnp.concatenate([mean, squares, mean, squares], axis=0)
    ref[...] = jnp.broadcast_to(jnp.transpose(both)[0:1][None], ref.shape)


def column(ref):
    return jnp.transpose(jnp.broadcast_to(ref[...], (128, ref.shape[1])))[:, :1]


def combine(stats, frame, channels, per_device):
    devices = lax.axis_size("tile")
    turned = jnp.transpose(stats[pl.ds(frame * devices, devices)].reshape(devices, 4 * GROUPS))
    mean, squares = turned[:GROUPS], turned[GROUPS : 2 * GROUPS]
    size = per_device * (channels // GROUPS)
    centre = jnp.sum(mean, axis=1, keepdims=True) / devices
    away = mean - centre
    total = jnp.sum(squares + size * (away * away), axis=1, keepdims=True)
    spread = lax.rsqrt(total / (devices * size) + EPS)
    lane = lax.broadcasted_iota(jnp.int32, (GROUPS, 128), 1)
    wide = exact(members(channels, True), jnp.where(lane == 0, centre, spread))
    return wide[:, 0:1], wide[:, 1:2]


def silu_norm(x, centre, scale, shift):
    half = 0.5 * ((x[...].astype(f32) - centre) * scale + shift)
    return half + half * jnp.tanh(half)


def put(ref, slot, row, x):
    channels, width = x.shape
    lane = lax.broadcasted_iota(jnp.int32, (channels, width), 1)
    x = x.astype(bf16)
    none = jnp.zeros((), bf16)
    left = jnp.where(lane == 0, none, pltpu.roll(x, 1, 1))
    right = jnp.where(lane == width - 1, none, pltpu.roll(x, width - 1, 1))
    base = row * 3 * channels
    ref[slot, base : base + channels] = left
    ref[slot, base + channels : base + 2 * channels] = x
    ref[slot, base + 2 * channels : base + 3 * channels] = right


def weights_kernel(coarse, up, fine, out_coarse, out_up, out_fine):
    c1, c2 = coarse.shape[3], fine.shape[3]
    for t in range(3):
        for a in range(3):
            for b in range(3):
                at = (a * 3 + b) * c1
                out_coarse[t, :, at : at + c1] = coarse[t, a, b]
    for b in range(3):
        first, second, third = (up[a, b].astype(f32) for a in range(3))
        at = b * c1
        for rows, a, value in (
            (0, 0, first + second),
            (0, 1, third),
            (1, 0, first),
            (1, 1, second + third),
        ):
            out_up[rows * c2 : (rows + 1) * c2, a * 3 * c1 + at : a * 3 * c1 + at + c1] = (
                value.astype(bf16)
            )
    out_fine[...] = jnp.zeros(out_fine.shape, bf16)
    for t in range(3):
        for a in range(3):
            for b in range(3):
                block = fine[t, a, b]
                for rho in range(2):
                    at = ((a + rho) * 3 + b) * c2
                    out_fine[t, rho * c2 : (rho + 1) * c2, at : at + c2] = block


CHUNKS = 4


def fold(ref, line):
    channels, width = line.shape
    ref[:channels] = line[:, : width // 2]
    ref[channels:] = line[:, width // 2 :]


def unfold(ref):
    channels = ref.shape[0] // 2
    return jnp.concatenate([ref[:channels], ref[channels:]], axis=1)


def fetches(source, target, arrived):
    part = source.shape[0] // CHUNKS
    cuts = [pl.ds(k * part, part) for k in range(CHUNKS)]
    return [
        pltpu.make_async_copy(source.at[cut], target.at[cut], arrived.at[k])
        for k, cut in enumerate(cuts)
    ]


def turn_kernel(
    latent, cache, fine, lat_t, cache_t, send, fine_v, lat_v, cache_v, lat_in, cache_in, fine_in
):
    lat_copies = fetches(latent, lat_v, lat_in)
    cache_copies = fetches(cache, cache_v, cache_in)
    fine_copies = fetches(fine, fine_v, fine_in)
    for copy in lat_copies + cache_copies + fine_copies:
        copy.start()
    for copy in lat_copies:
        copy.wait()
    lat_t[...] = jnp.swapaxes(lat_v[...], 0, 1)
    for copy in cache_copies:
        copy.wait()
    cache_t[...] = jnp.swapaxes(cache_v[...], 0, 1)

    @pl.when(lax.axis_index("tm") == 0)
    def _():
        send[...] = lat_t[...]

    @pl.when(lax.axis_index("tm") != 0)
    def _():
        send[...] = cache_t[...]

    for copy in fine_copies:
        copy.wait()


def moments_kernel(lat_t, cache_t, fine, pay, fine_t, up, down):
    rows, _, width = lat_t.shape
    fine_t[...] = jnp.swapaxes(fine[...], 0, 1)
    for ref, cut, line in (
        (up, slice(rows - 2, rows), fine_t[2 * rows - 1]),
        (down, slice(0, 2), fine_t[0]),
    ):
        ref[0:2] = lat_t[cut]
        ref[2:4] = cache_t[cut]
        fold(ref.at[4], line)
    payload(pay, *moments([lat_t[r] for r in range(rows)], rows * width))


def coarse_first(cache_t, above, below, weights, acc, stack):
    rows, channels, width = cache_t.shape
    for r in range(2):
        put(stack, 0, r, above[2 + r])
        put(stack, 0, rows + 2 + r, below[2 + r])
    for r in range(rows):
        put(stack, 0, 2 + r, cache_t[r])
    step = 3 * channels
    for r in range(rows + 2):
        acc[r] = dot(weights[0], stack[0, r * step : (r + 3) * step])


def put_normed(stack, middle, above, below, stats, frame, gain, shift):
    tile = lax.axis_index("tile")
    last = lax.axis_size("tile") - 1
    rows, (channels, width) = len(middle), middle[0].shape
    centre, spread = combine(stats, frame, channels, rows * width)
    scale, offset = spread * column(gain), column(shift)
    top = jnp.where(tile == 0, 0.0, 1.0)
    bottom = jnp.where(tile == last, 0.0, 1.0)
    for r in range(2):
        put(stack, 0, r, silu_norm(above[r], centre, scale, offset) * top)
        put(stack, 0, rows + 2 + r, silu_norm(below[r], centre, scale, offset) * bottom)
    for r in range(rows):
        put(stack, 0, 2 + r, silu_norm(middle[r], centre, scale, offset))


def rows_of(*refs):
    return [ref.at[r] for ref in refs for r in range(ref.shape[0])]


def coarse_third(lat_t, above, below, stats, gain, shift, weights, acc, out, stack):
    frame = lax.axis_index("tm")
    put_normed(
        stack, rows_of(lat_t), rows_of(above), rows_of(below), stats, frame, gain, shift
    )
    rows, channels, _ = lat_t.shape
    step = 3 * channels
    for r in range(rows + 2):
        out[r] = acc[r] + dot(weights[2], stack[0, r * step : (r + 3) * step])


def coarse_second(
    other, above, below, stats, gain, shift, weights, acc, out, rims, stack
):
    frame = lax.axis_index("tm")
    tile = lax.axis_index("tile")
    last = lax.axis_size("tile") - 1
    rows, channels, _ = other.shape
    other, above, below = rows_of(other), rows_of(above), rows_of(below)

    @pl.when(frame == 0)
    def _():
        for r, ref in enumerate(above + other + below):
            put(stack, 0, r, ref[...])

    @pl.when(frame != 0)
    def _():
        put_normed(stack, other, above, below, stats, 0, gain, shift)

    step = 3 * channels
    for r in range(rows + 2):
        value = acc[r] + dot(weights[1], stack[0, r * step : (r + 3) * step])
        if r == 0:
            value = value * jnp.where(tile == 0, 0.0, 1.0)
        if r == rows + 1:
            value = value * jnp.where(tile == last, 0.0, 1.0)
        target = rims.at[r // rows] if r in (0, rows + 1) else out.at[r - 1]
        target[...] = value.astype(bf16)


def raise_rows(coarse, weights, raised, stack):
    rows, (channels, width) = len(coarse), coarse[0].shape
    row = lax.broadcasted_iota(jnp.int32, (width, 2 * width), 0)
    col = lax.broadcasted_iota(jnp.int32, (width, 2 * width), 1) // 2
    spread_out = (row == col).astype(f32).astype(bf16)
    for r in range(rows):
        put(stack, 0, r, dot(coarse[r][...], spread_out))
    step = 3 * channels
    c2 = weights.shape[0] // 2
    for m in range(rows - 1):
        both = dot(weights[...], stack[0, m * step : (m + 2) * step]).astype(bf16)
        raised[2 * m] = both[:c2]
        raised[2 * m + 1] = both[c2:]


def up_kernel(coarse, rims, above, below, weights, raised, pay, late, stack):
    frame = lax.axis_index("tm")

    @pl.when(frame == 0)
    def _():
        late[...] = rims[...]

    @pl.when(frame != 0)
    def _():
        late[0] = above[4]
        late[1] = below[4]

    raise_rows([rims.at[0], *rows_of(coarse), rims.at[1]], weights, raised, stack)
    count = raised.shape[0] - 2
    payload(pay, *moments([raised[r + 1] for r in range(count)], count * raised.shape[2]))


def put_active(stack, raised, stats, frame, gain, shift):
    tile = lax.axis_index("tile")
    last = lax.axis_size("tile") - 1
    rows, (channels, width) = len(raised), raised[0].shape
    centre, spread = combine(stats, frame, channels, (rows - 2) * width)
    scale, offset = spread * column(gain), column(shift)
    for r in range(rows):
        value = silu_norm(raised[r], centre, scale, offset)
        if r == 0:
            value = value * jnp.where(tile == 0, 0.0, 1.0)
        if r == rows - 1:
            value = value * jnp.where(tile == last, 0.0, 1.0)
        put(stack, 0, r, value)


def put_rims(stack, last, above, below):
    put(stack, 0, 0, unfold(above))
    put(stack, 0, last, unfold(below))


def put_cache(stack, fine_t):
    for r in range(fine_t.shape[0]):
        put(stack, 0, 1 + r, fine_t[r])


def fine_window(stack, m, step):
    return stack[0, 2 * m * step : (2 * m + 4) * step]


def fine_first(fine_t, above, below, weights, acc, stack):
    put_rims(stack, fine_t.shape[0] + 1, above.at[4], below.at[4])
    put_cache(stack, fine_t)
    for m in range(acc.shape[0]):
        acc[m] = dot(weights[0], fine_window(stack, m, 3 * fine_t.shape[1]))


def fine_third(raised, stats, gain, shift, weights, acc, out, stack):
    put_active(stack, rows_of(raised), stats, lax.axis_index("tm"), gain, shift)
    for m in range(acc.shape[0]):
        out[m] = acc[m] + dot(weights[2], fine_window(stack, m, 3 * raised.shape[1]))


def fine_begin(fine_r, coarse, weights, raised, stack, stack_up):
    frame = lax.axis_index("tm")

    @pl.when(frame == 0)
    def _():
        put_cache(stack, fine_r)

    @pl.when(frame != 0)
    def _():
        raise_rows(rows_of(coarse), weights, raised, stack_up)


def fine_end(begun, coarse, late, raised, stats, gain, shift, weights, stack, ends, stack_up):
    frame = lax.axis_index("tm")

    @pl.when(frame == 0)
    def _():
        put_rims(stack, 2 * coarse.shape[0] + 1, late.at[0], late.at[1])

    @pl.when(frame != 0)
    def _():
        top, bottom = ends.at[0:2], ends.at[2:4]
        raise_rows([late.at[0], coarse.at[0]], weights, top, stack_up)
        raise_rows([coarse.at[coarse.shape[0] - 1], late.at[1]], weights, bottom, stack_up)
        put_active(stack, rows_of(top, raised, bottom), stats, 0, gain, shift)


def fine_second(stack, bias, weights, acc, out, turned):
    c2 = out.shape[0]
    offset = column(bias)
    for m in range(acc.shape[0]):
        both = acc[m] + dot(weights[1], fine_window(stack, m, 3 * c2))
        turned[2 * m] = (both[:c2] + offset).astype(bf16)
        turned[2 * m + 1] = (both[c2:] + offset).astype(bf16)
    out[...] = jnp.swapaxes(turned[...], 0, 1)


def per_device(
    latent,
    coarse_cache,
    fine_cache,
    gain_coarse,
    shift_coarse,
    weight_coarse,
    weight_up,
    gain_fine,
    shift_fine,
    weight_fine,
    bias_fine,
):
    _, c1, rows, cols = latent.shape
    c2 = fine_cache.shape[1]
    tiles = lax.axis_size("tile")
    fine_rows, fine_cols = 2 * rows, 2 * cols
    forward = [(i, i + 1) for i in range(tiles - 1)]
    backward = [(i + 1, i) for i in range(tiles - 1)]
    later, earlier = [(0, 1)], [(1, 0)]
    gain_coarse, shift_coarse = gain_coarse[None], shift_coarse[None]
    gain_fine, shift_fine, bias_fine = gain_fine[None], shift_fine[None], bias_fine[None]

    def shared(stats):
        return lax.all_to_all(stats, ("tm", "tile"), 0, 0)

    def after(value, *others):
        return lax.optimization_barrier((value, *others))[0]

    devices = lax.axis_size("tm") * tiles
    coarse_shape, coarse_acc = (rows, c1, cols), ((rows + 2, c1, cols), f32)
    fine_acc = ((rows, 2 * c2, fine_cols), f32)
    coarse_stack = pltpu.VMEM((1, (rows + 4) * 3 * c1, cols), bf16)
    stack_shape = ((1, (fine_rows + 2) * 3 * c2, fine_cols), bf16)
    fine_scratch = pltpu.VMEM(*stack_shape)
    up_stack = pltpu.VMEM((1, (rows + 2) * 3 * c1, fine_cols), bf16)
    raised_shape = ((fine_rows + 2, c2, fine_cols), bf16)

    rim = ((5, c1, cols), bf16)
    fine_raw = ((c2, fine_rows, fine_cols), bf16)
    lat_t, cache_t, send, fine_v = call(
        turn_kernel,
        "turn",
        [(coarse_shape, bf16)] * 3 + [fine_raw],
        [pltpu.VMEM((c1, rows, cols), bf16)] * 2 + [pltpu.SemaphoreType.DMA((CHUNKS,))] * 3,
        far=3,
    )(latent[0], coarse_cache[0], fine_cache[0])
    other = lax.ppermute(send, "tm", [(0, 1), (1, 0)])
    pay, fine_t, rim_up, rim_down = call(
        moments_kernel,
        "moments",
        [((devices, 1, 4 * GROUPS), f32), ((fine_rows, c2, fine_cols), bf16)] + [rim] * 2,
    )(lat_t, cache_t, fine_v)
    above = lax.ppermute(rim_up, "tile", forward)
    below = lax.ppermute(rim_down, "tile", backward)
    w_coarse, w_up, w_fine = call(
        weights_kernel,
        "weights",
        [((3, c1, 9 * c1), bf16), ((2 * c2, 6 * c1), bf16), ((3, 2 * c2, 12 * c2), bf16)],
    )(weight_coarse, weight_up, weight_fine)
    stats = shared(after(pay, w_coarse))
    stats, other, above, below = lax.optimization_barrier((stats, other, above, below))
    (acc,) = call(coarse_first, "coarse_first", [coarse_acc], [coarse_stack])(
        cache_t, above, below, w_coarse
    )
    other_above = lax.ppermute(other[rows - 2 :], "tile", forward)
    other_below = lax.ppermute(other[:2], "tile", backward)
    (acc,) = call(coarse_third, "coarse_third", [coarse_acc], [coarse_stack])(
        lat_t,
        above,
        below,
        stats,
        gain_coarse,
        shift_coarse,
        w_coarse,
        after(acc, other_above, other_below),
    )
    fine_r = lax.ppermute(after(fine_t, other_above, other_below), "tm", earlier)
    coarse, coarse_rims = call(
        coarse_second,
        "coarse_second",
        [(coarse_shape, bf16), ((2, c1, cols), bf16)],
        [coarse_stack],
    )(other, other_above, other_below, stats, gain_coarse, shift_coarse, w_coarse, acc)
    coarse_r = lax.ppermute(coarse, "tm", later)
    raised, pay, late = call(
        up_kernel,
        "up",
        [raised_shape, ((devices, 1, 4 * GROUPS), f32), ((2, c1, cols), bf16)],
        [up_stack],
    )(coarse, coarse_rims, above, below, w_up)
    (acc,) = call(fine_first, "fine_first", [fine_acc], [fine_scratch])(
        fine_t, above, below, w_fine
    )

    stats = shared(after(pay, acc))
    stats, fine_r, coarse_r = lax.optimization_barrier((stats, fine_r, coarse_r))
    late = lax.ppermute(after(late, stats), "tm", [(0, 1), (1, 0)])
    raised_r, stack = call(
        fine_begin,
        "fine_begin",
        [((fine_rows - 2, c2, fine_cols), bf16), stack_shape],
        [up_stack],
    )(fine_r, coarse_r, w_up)
    (acc,) = call(fine_third, "fine_third", [fine_acc], [fine_scratch])(
        raised, stats, gain_fine, shift_fine, w_fine, acc
    )
    (stack,) = call(
        fine_end,
        "fine_end",
        [stack_shape],
        [pltpu.VMEM((4, c2, fine_cols), bf16), up_stack],
        aliases={0: 0},
    )(stack, coarse_r, late, raised_r, stats, gain_fine, shift_fine, w_up)
    (out,) = call(
        fine_second,
        "fine_second",
        [fine_raw],
        [pltpu.VMEM((fine_rows, c2, fine_cols), bf16)],
        local=False,
    )(stack, bias_fine, w_fine, acc)
    return out[None]


def solution(mesh):
    split = P("tm", None, "tile", None)
    return jax.shard_map(
        per_device,
        mesh=mesh,
        in_specs=(split,) * 3 + (P(),) * 8,
        out_specs=split,
        check_vma=False,
    )
```

```python
import jax
import jax.numpy as jnp
from jax import lax
from jax.experimental import pallas as pl
from jax.experimental.pallas import tpu as pltpu
from jax.sharding import PartitionSpec as P

GROUPS = 32
EPS = 1e-05
f32 = jnp.float32
bf16 = jnp.bfloat16


def call(kernel, name, outs, scratch=(), local=True, limit=12, far=0, aliases=None):
    def with_arrays(*arrays):
        near = [pltpu.with_memory_space_constraint(a, pltpu.VMEM) for a in arrays[far:]]
        away = [pltpu.with_memory_space_constraint(a, pltpu.HBM) for a in arrays[:far]]
        return pl.pallas_call(
            kernel,
            in_specs=[pl.BlockSpec(memory_space=pltpu.HBM)] * far
            + [pl.BlockSpec(memory_space=pltpu.VMEM)] * len(near),
            out_shape=[pltpu.VMEM(s, d) if local else jax.ShapeDtypeStruct(s, d) for s, d in outs],
            scratch_shapes=list(scratch),
            input_output_aliases=aliases or {},
            compiler_params=pltpu.CompilerParams(vmem_limit_bytes=limit * 2**20),
            name=name,
        )(*away, *near)

    return with_arrays


def dot(a, b):
    return jnp.dot(a, b, preferred_element_type=f32)


def exact(a, b):
    return jnp.dot(a, b, preferred_element_type=f32, precision=lax.Precision.HIGHEST)


def members(channels, transposed=False):
    shape, dim = ((channels, GROUPS), 1) if transposed else ((GROUPS, channels), 0)
    group = lax.broadcasted_iota(jnp.int32, shape, dim)
    channel = lax.broadcasted_iota(jnp.int32, shape, 1 - dim)
    return (group == channel // (channels // GROUPS)).astype(f32)


def moments(rows, count):
    channels = rows[0].shape[0]
    total = rows[0].astype(f32)
    for row in rows[1:]:
        total = total + row.astype(f32)
    total = jnp.broadcast_to(jnp.sum(total, axis=1, keepdims=True), (channels, 128))
    mean = exact(members(channels), total) / (count * (channels // GROUPS))
    centre = exact(members(channels, True), mean)[:, :1]
    squares = None
    for row in rows:
        centred = row.astype(f32) - centre
        squares = centred * centred if squares is None else squares + centred * centred
    squares = jnp.broadcast_to(jnp.sum(squares, axis=1, keepdims=True), (channels, 128))
    return mean, exact(members(channels), squares)


def payload(ref, mean, squares):
    both = jnp.concatenate([mean, squares, mean, squares], axis=0)
    ref[...] = jnp.broadcast_to(jnp.transpose(both)[0:1][None], ref.shape)


def column(ref):
    return jnp.transpose(jnp.broadcast_to(ref[...], (128, ref.shape[1])))[:, :1]


def combine(stats, frame, channels, per_device):
    devices = lax.axis_size("tile")
    turned = jnp.transpose(stats[pl.ds(frame * devices, devices)].reshape(devices, 4 * GROUPS))
    mean, squares = turned[:GROUPS], turned[GROUPS : 2 * GROUPS]
    size = per_device * (channels // GROUPS)
    centre = jnp.sum(mean, axis=1, keepdims=True) / devices
    away = mean - centre
    total = jnp.sum(squares + size * (away * away), axis=1, keepdims=True)
    spread = lax.rsqrt(total / (devices * size) + EPS)
    lane = lax.broadcasted_iota(jnp.int32, (GROUPS, 128), 1)
    wide = exact(members(channels, True), jnp.where(lane == 0, centre, spread))
    return wide[:, 0:1], wide[:, 1:2]


def silu_norm(x, centre, scale, shift):
    half = 0.5 * ((x[...].astype(f32) - centre) * scale + shift)
    return half + half * jnp.tanh(half)


def put(ref, slot, row, x):
    channels, width = x.shape
    lane = lax.broadcasted_iota(jnp.int32, (channels, width), 1)
    x = x.astype(bf16)
    none = jnp.zeros((), bf16)
    left = jnp.where(lane == 0, none, pltpu.roll(x, 1, 1))
    right = jnp.where(lane == width - 1, none, pltpu.roll(x, width - 1, 1))
    base = row * 3 * channels
    ref[slot, base : base + channels] = left
    ref[slot, base + channels : base + 2 * channels] = x
    ref[slot, base + 2 * channels : base + 3 * channels] = right


def weights_kernel(coarse, up, fine, out_coarse, out_up, out_fine):
    c1, c2 = coarse.shape[3], fine.shape[3]
    for t in range(3):
        for a in range(3):
            for b in range(3):
                at = (a * 3 + b) * c1
                out_coarse[t, :, at : at + c1] = coarse[t, a, b]
    for b in range(3):
        first, second, third = (up[a, b].astype(f32) for a in range(3))
        at = b * c1
        for rows, a, value in (
            (0, 0, first + second),
            (0, 1, third),
            (1, 0, first),
            (1, 1, second + third),
        ):
            out_up[rows * c2 : (rows + 1) * c2, a * 3 * c1 + at : a * 3 * c1 + at + c1] = (
                value.astype(bf16)
            )
    out_fine[...] = jnp.zeros(out_fine.shape, bf16)
    for t in range(3):
        for a in range(3):
            for b in range(3):
                block = fine[t, a, b]
                for rho in range(2):
                    at = ((a + rho) * 3 + b) * c2
                    out_fine[t, rho * c2 : (rho + 1) * c2, at : at + c2] = block


CHUNKS = 4


def fold(ref, line):
    channels, width = line.shape
    ref[:channels] = line[:, : width // 2]
    ref[channels:] = line[:, width // 2 :]


def unfold(ref):
    channels = ref.shape[0] // 2
    return jnp.concatenate([ref[:channels], ref[channels:]], axis=1)


def fetches(source, target, arrived):
    part = source.shape[0] // CHUNKS
    cuts = [pl.ds(k * part, part) for k in range(CHUNKS)]
    return [
        pltpu.make_async_copy(source.at[cut], target.at[cut], arrived.at[k])
        for k, cut in enumerate(cuts)
    ]


def turn_kernel(
    latent, cache, fine, lat_t, cache_t, send, fine_v, lat_v, cache_v, lat_in, cache_in, fine_in
):
    lat_copies = fetches(latent, lat_v, lat_in)
    cache_copies = fetches(cache, cache_v, cache_in)
    fine_copies = fetches(fine, fine_v, fine_in)
    for copy in lat_copies + cache_copies + fine_copies:
        copy.start()
    for copy in lat_copies:
        copy.wait()
    lat_t[...] = jnp.swapaxes(lat_v[...], 0, 1)
    for copy in cache_copies:
        copy.wait()
    cache_t[...] = jnp.swapaxes(cache_v[...], 0, 1)

    @pl.when(lax.axis_index("tm") == 0)
    def _():
        send[...] = lat_t[...]

    @pl.when(lax.axis_index("tm") != 0)
    def _():
        send[...] = cache_t[...]

    for copy in fine_copies:
        copy.wait()


def moments_kernel(lat_t, cache_t, fine, pay, fine_t, up, down):
    rows, _, width = lat_t.shape
    fine_t[...] = jnp.swapaxes(fine[...], 0, 1)
    for ref, cut, line in (
        (up, slice(rows - 2, rows), fine_t[2 * rows - 1]),
        (down, slice(0, 2), fine_t[0]),
    ):
        ref[0:2] = lat_t[cut]
        ref[2:4] = cache_t[cut]
        fold(ref.at[4], line)
    payload(pay, *moments([lat_t[r] for r in range(rows)], rows * width))


def coarse_first(cache_t, above, below, weights, acc, stack):
    rows, channels, width = cache_t.shape
    for r in range(2):
        put(stack, 0, r, above[2 + r])
        put(stack, 0, rows + 2 + r, below[2 + r])
    for r in range(rows):
        put(stack, 0, 2 + r, cache_t[r])
    step = 3 * channels
    for r in range(rows + 2):
        acc[r] = dot(weights[0], stack[0, r * step : (r + 3) * step])


def put_normed(stack, middle, above, below, stats, frame, gain, shift):
    tile = lax.axis_index("tile")
    last = lax.axis_size("tile") - 1
    rows, (channels, width) = len(middle), middle[0].shape
    centre, spread = combine(stats, frame, channels, rows * width)
    scale, offset = spread * column(gain), column(shift)
    top = jnp.where(tile == 0, 0.0, 1.0)
    bottom = jnp.where(tile == last, 0.0, 1.0)
    for r in range(2):
        put(stack, 0, r, silu_norm(above[r], centre, scale, offset) * top)
        put(stack, 0, rows + 2 + r, silu_norm(below[r], centre, scale, offset) * bottom)
    for r in range(rows):
        put(stack, 0, 2 + r, silu_norm(middle[r], centre, scale, offset))


def rows_of(*refs):
    return [ref.at[r] for ref in refs for r in range(ref.shape[0])]


def coarse_third(lat_t, above, below, stats, gain, shift, weights, acc, out, stack):
    frame = lax.axis_index("tm")
    put_normed(
        stack, rows_of(lat_t), rows_of(above), rows_of(below), stats, frame, gain, shift
    )
    rows, channels, _ = lat_t.shape
    step = 3 * channels
    for r in range(rows + 2):
        out[r] = acc[r] + dot(weights[2], stack[0, r * step : (r + 3) * step])


def coarse_second(
    other, above, below, stats, gain, shift, weights, acc, out, rims, stack
):
    frame = lax.axis_index("tm")
    tile = lax.axis_index("tile")
    last = lax.axis_size("tile") - 1
    rows, channels, _ = other.shape
    other, above, below = rows_of(other), rows_of(above), rows_of(below)

    @pl.when(frame == 0)
    def _():
        for r, ref in enumerate(above + other + below):
            put(stack, 0, r, ref[...])

    @pl.when(frame != 0)
    def _():
        put_normed(stack, other, above, below, stats, 0, gain, shift)

    step = 3 * channels
    for r in range(rows + 2):
        value = acc[r] + dot(weights[1], stack[0, r * step : (r + 3) * step])
        if r == 0:
            value = value * jnp.where(tile == 0, 0.0, 1.0)
        if r == rows + 1:
            value = value * jnp.where(tile == last, 0.0, 1.0)
        target = rims.at[r // rows] if r in (0, rows + 1) else out.at[r - 1]
        target[...] = value.astype(bf16)


def raise_rows(coarse, weights, raised, stack):
    rows, (channels, width) = len(coarse), coarse[0].shape
    row = lax.broadcasted_iota(jnp.int32, (width, 2 * width), 0)
    col = lax.broadcasted_iota(jnp.int32, (width, 2 * width), 1) // 2
    spread_out = (row == col).astype(f32).astype(bf16)
    for r in range(rows):
        put(stack, 0, r, dot(coarse[r][...], spread_out))
    step = 3 * channels
    c2 = weights.shape[0] // 2
    for m in range(rows - 1):
        both = dot(weights[...], stack[0, m * step : (m + 2) * step]).astype(bf16)
        raised[2 * m] = both[:c2]
        raised[2 * m + 1] = both[c2:]


def up_kernel(coarse, rims, above, below, weights, raised, pay, late, stack):
    frame = lax.axis_index("tm")

    @pl.when(frame == 0)
    def _():
        late[...] = rims[...]

    @pl.when(frame != 0)
    def _():
        late[0] = above[4]
        late[1] = below[4]

    raise_rows([rims.at[0], *rows_of(coarse), rims.at[1]], weights, raised, stack)
    count = raised.shape[0] - 2
    payload(pay, *moments([raised[r + 1] for r in range(count)], count * raised.shape[2]))


def put_active(stack, raised, stats, frame, gain, shift):
    tile = lax.axis_index("tile")
    last = lax.axis_size("tile") - 1
    rows, (channels, width) = len(raised), raised[0].shape
    centre, spread = combine(stats, frame, channels, (rows - 2) * width)
    scale, offset = spread * column(gain), column(shift)
    for r in range(rows):
        value = silu_norm(raised[r], centre, scale, offset)
        if r == 0:
            value = value * jnp.where(tile == 0, 0.0, 1.0)
        if r == rows - 1:
            value = value * jnp.where(tile == last, 0.0, 1.0)
        put(stack, 0, r, value)


def put_rims(stack, last, above, below):
    put(stack, 0, 0, unfold(above))
    put(stack, 0, last, unfold(below))


def put_cache(stack, fine_t):
    for r in range(fine_t.shape[0]):
        put(stack, 0, 1 + r, fine_t[r])


def fine_window(stack, m, step):
    return stack[0, 2 * m * step : (2 * m + 4) * step]


def fine_first(fine_t, above, below, weights, acc, stack):
    put_rims(stack, fine_t.shape[0] + 1, above.at[4], below.at[4])
    put_cache(stack, fine_t)
    for m in range(acc.shape[0]):
        acc[m] = dot(weights[0], fine_window(stack, m, 3 * fine_t.shape[1]))


def fine_third(raised, stats, gain, shift, weights, acc, out, stack):
    put_active(stack, rows_of(raised), stats, lax.axis_index("tm"), gain, shift)
    for m in range(acc.shape[0]):
        out[m] = acc[m] + dot(weights[2], fine_window(stack, m, 3 * raised.shape[1]))


def fine_begin(coarse, weights, raised, stack_up):
    @pl.when(lax.axis_index("tm") != 0)
    def _():
        raise_rows(rows_of(coarse), weights, raised, stack_up)


def fine_end(fine_r, coarse, late, raised, stats, gain, shift, weights, stack, ends, stack_up):
    frame = lax.axis_index("tm")

    @pl.when(frame == 0)
    def _():
        put_cache(stack, fine_r)
        put_rims(stack, 2 * coarse.shape[0] + 1, late.at[0], late.at[1])

    @pl.when(frame != 0)
    def _():
        top, bottom = ends.at[0:2], ends.at[2:4]
        raise_rows([late.at[0], coarse.at[0]], weights, top, stack_up)
        raise_rows([coarse.at[coarse.shape[0] - 1], late.at[1]], weights, bottom, stack_up)
        put_active(stack, rows_of(top, raised, bottom), stats, 0, gain, shift)


def fine_second(stack, bias, weights, acc, out, turned):
    c2 = out.shape[0]
    offset = column(bias)
    for m in range(acc.shape[0]):
        both = acc[m] + dot(weights[1], fine_window(stack, m, 3 * c2))
        turned[2 * m] = (both[:c2] + offset).astype(bf16)
        turned[2 * m + 1] = (both[c2:] + offset).astype(bf16)
    out[...] = jnp.swapaxes(turned[...], 0, 1)


def per_device(
    latent,
    coarse_cache,
    fine_cache,
    gain_coarse,
    shift_coarse,
    weight_coarse,
    weight_up,
    gain_fine,
    shift_fine,
    weight_fine,
    bias_fine,
):
    _, c1, rows, cols = latent.shape
    c2 = fine_cache.shape[1]
    tiles = lax.axis_size("tile")
    fine_rows, fine_cols = 2 * rows, 2 * cols
    forward = [(i, i + 1) for i in range(tiles - 1)]
    backward = [(i + 1, i) for i in range(tiles - 1)]
    later, earlier = [(0, 1)], [(1, 0)]
    gain_coarse, shift_coarse = gain_coarse[None], shift_coarse[None]
    gain_fine, shift_fine, bias_fine = gain_fine[None], shift_fine[None], bias_fine[None]

    def shared(stats):
        return lax.all_to_all(stats, ("tm", "tile"), 0, 0)

    def after(value, *others):
        return lax.optimization_barrier((value, *others))[0]

    devices = lax.axis_size("tm") * tiles
    coarse_shape, coarse_acc = (rows, c1, cols), ((rows + 2, c1, cols), f32)
    fine_acc = ((rows, 2 * c2, fine_cols), f32)
    coarse_stack = pltpu.VMEM((1, (rows + 4) * 3 * c1, cols), bf16)
    stack_shape = ((1, (fine_rows + 2) * 3 * c2, fine_cols), bf16)
    fine_scratch = pltpu.VMEM(*stack_shape)
    up_stack = pltpu.VMEM((1, (rows + 2) * 3 * c1, fine_cols), bf16)
    raised_shape = ((fine_rows + 2, c2, fine_cols), bf16)

    rim = ((5, c1, cols), bf16)
    fine_raw = ((c2, fine_rows, fine_cols), bf16)
    lat_t, cache_t, send, fine_v = call(
        turn_kernel,
        "turn",
        [(coarse_shape, bf16)] * 3 + [fine_raw],
        [pltpu.VMEM((c1, rows, cols), bf16)] * 2 + [pltpu.SemaphoreType.DMA((CHUNKS,))] * 3,
        far=3,
    )(latent[0], coarse_cache[0], fine_cache[0])
    other = lax.ppermute(send, "tm", [(0, 1), (1, 0)])
    pay, fine_t, rim_up, rim_down = call(
        moments_kernel,
        "moments",
        [((devices, 1, 4 * GROUPS), f32), ((fine_rows, c2, fine_cols), bf16)] + [rim] * 2,
    )(lat_t, cache_t, fine_v)
    above = lax.ppermute(rim_up, "tile", forward)
    below = lax.ppermute(rim_down, "tile", backward)
    w_coarse, w_up, w_fine = call(
        weights_kernel,
        "weights",
        [((3, c1, 9 * c1), bf16), ((2 * c2, 6 * c1), bf16), ((3, 2 * c2, 12 * c2), bf16)],
    )(weight_coarse, weight_up, weight_fine)
    stats = shared(after(pay, w_coarse))
    stats, other, above, below = lax.optimization_barrier((stats, other, above, below))
    (first,) = call(coarse_first, "coarse_first", [coarse_acc], [coarse_stack])(
        cache_t, above, below, w_coarse
    )
    other_above = lax.ppermute(other[rows - 2 :], "tile", forward)
    other_below = lax.ppermute(other[:2], "tile", backward)
    (acc,) = call(coarse_third, "coarse_third", [coarse_acc], [coarse_stack])(
        lat_t,
        above,
        below,
        stats,
        gain_coarse,
        shift_coarse,
        w_coarse,
        after(first, other_above, other_below),
    )
    fine_r = lax.ppermute(after(fine_t, first, other_above, other_below), "tm", earlier)
    coarse, coarse_rims = call(
        coarse_second,
        "coarse_second",
        [(coarse_shape, bf16), ((2, c1, cols), bf16)],
        [coarse_stack],
    )(other, other_above, other_below, stats, gain_coarse, shift_coarse, w_coarse, acc)
    coarse_r = lax.ppermute(coarse, "tm", later)
    raised, pay, late = call(
        up_kernel,
        "up",
        [raised_shape, ((devices, 1, 4 * GROUPS), f32), ((2, c1, cols), bf16)],
        [up_stack],
    )(coarse, coarse_rims, above, below, w_up)
    (acc,) = call(fine_first, "fine_first", [fine_acc], [fine_scratch])(
        fine_t, above, below, w_fine
    )

    stats = shared(after(pay, acc))
    stats, fine_r, coarse_r = lax.optimization_barrier((stats, fine_r, coarse_r))
    (raised_r,) = call(
        fine_begin, "fine_begin", [((fine_rows - 2, c2, fine_cols), bf16)], [up_stack]
    )(coarse_r, w_up)
    late = lax.ppermute(after(late, raised_r), "tm", [(0, 1), (1, 0)])
    (acc,) = call(fine_third, "fine_third", [fine_acc], [fine_scratch])(
        raised, stats, gain_fine, shift_fine, w_fine, acc
    )
    (stack,) = call(
        fine_end, "fine_end", [stack_shape], [pltpu.VMEM((4, c2, fine_cols), bf16), up_stack]
    )(fine_r, coarse_r, late, raised_r, stats, gain_fine, shift_fine, w_up)
    (out,) = call(
        fine_second,
        "fine_second",
        [fine_raw],
        [pltpu.VMEM((fine_rows, c2, fine_cols), bf16)],
        local=False,
    )(stack, bias_fine, w_fine, acc)
    return out[None]


def solution(mesh):
    split = P("tm", None, "tile", None)
    return jax.shard_map(
        per_device,
        mesh=mesh,
        in_specs=(split,) * 3 + (P(),) * 8,
        out_specs=split,
        check_vma=False,
    )
```

```python
import jax
import jax.numpy as jnp
from jax import lax
from jax.experimental import pallas as pl
from jax.experimental.pallas import tpu as pltpu
from jax.sharding import PartitionSpec as P

GROUPS = 32
EPS = 1e-05
f32 = jnp.float32
bf16 = jnp.bfloat16


def call(kernel, name, outs, scratch=(), local=True, limit=12, far=0, aliases=None):
    def with_arrays(*arrays):
        near = [pltpu.with_memory_space_constraint(a, pltpu.VMEM) for a in arrays[far:]]
        away = [pltpu.with_memory_space_constraint(a, pltpu.HBM) for a in arrays[:far]]
        return pl.pallas_call(
            kernel,
            in_specs=[pl.BlockSpec(memory_space=pltpu.HBM)] * far
            + [pl.BlockSpec(memory_space=pltpu.VMEM)] * len(near),
            out_shape=[pltpu.VMEM(s, d) if local else jax.ShapeDtypeStruct(s, d) for s, d in outs],
            scratch_shapes=list(scratch),
            input_output_aliases=aliases or {},
            compiler_params=pltpu.CompilerParams(vmem_limit_bytes=limit * 2**20),
            name=name,
        )(*away, *near)

    return with_arrays


def dot(a, b):
    return jnp.dot(a, b, preferred_element_type=f32)


def exact(a, b):
    return jnp.dot(a, b, preferred_element_type=f32, precision=lax.Precision.HIGHEST)


def members(channels, transposed=False):
    shape, dim = ((channels, GROUPS), 1) if transposed else ((GROUPS, channels), 0)
    group = lax.broadcasted_iota(jnp.int32, shape, dim)
    channel = lax.broadcasted_iota(jnp.int32, shape, 1 - dim)
    return (group == channel // (channels // GROUPS)).astype(f32)


def moments(rows, count):
    channels = rows[0].shape[0]
    total = rows[0].astype(f32)
    for row in rows[1:]:
        total = total + row.astype(f32)
    total = jnp.broadcast_to(jnp.sum(total, axis=1, keepdims=True), (channels, 128))
    mean = exact(members(channels), total) / (count * (channels // GROUPS))
    centre = exact(members(channels, True), mean)[:, :1]
    squares = None
    for row in rows:
        centred = row.astype(f32) - centre
        squares = centred * centred if squares is None else squares + centred * centred
    squares = jnp.broadcast_to(jnp.sum(squares, axis=1, keepdims=True), (channels, 128))
    return mean, exact(members(channels), squares)


def payload(ref, mean, squares):
    both = jnp.concatenate([mean, squares, mean, squares], axis=0)
    ref[...] = jnp.broadcast_to(jnp.transpose(both)[0:1][None], ref.shape)


def column(ref):
    return jnp.transpose(jnp.broadcast_to(ref[...], (128, ref.shape[1])))[:, :1]


def combine(stats, frame, channels, per_device):
    devices = lax.axis_size("tile")
    turned = jnp.transpose(stats[pl.ds(frame * devices, devices)].reshape(devices, 4 * GROUPS))
    mean, squares = turned[:GROUPS], turned[GROUPS : 2 * GROUPS]
    size = per_device * (channels // GROUPS)
    centre = jnp.sum(mean, axis=1, keepdims=True) / devices
    away = mean - centre
    total = jnp.sum(squares + size * (away * away), axis=1, keepdims=True)
    spread = lax.rsqrt(total / (devices * size) + EPS)
    lane = lax.broadcasted_iota(jnp.int32, (GROUPS, 128), 1)
    wide = exact(members(channels, True), jnp.where(lane == 0, centre, spread))
    return wide[:, 0:1], wide[:, 1:2]


def silu_norm(x, centre, scale, shift):
    half = 0.5 * ((x[...].astype(f32) - centre) * scale + shift)
    return half + half * jnp.tanh(half)


def put(ref, slot, row, x):
    channels, width = x.shape
    lane = lax.broadcasted_iota(jnp.int32, (channels, width), 1)
    x = x.astype(bf16)
    none = jnp.zeros((), bf16)
    left = jnp.where(lane == 0, none, pltpu.roll(x, 1, 1))
    right = jnp.where(lane == width - 1, none, pltpu.roll(x, width - 1, 1))
    base = row * 3 * channels
    ref[slot, base : base + channels] = left
    ref[slot, base + channels : base + 2 * channels] = x
    ref[slot, base + 2 * channels : base + 3 * channels] = right


def weights_kernel(coarse, up, fine, out_coarse, out_up, out_fine):
    c1, c2 = coarse.shape[3], fine.shape[3]
    for t in range(3):
        for a in range(3):
            for b in range(3):
                at = (a * 3 + b) * c1
                out_coarse[t, :, at : at + c1] = coarse[t, a, b]
    for b in range(3):
        first, second, third = (up[a, b].astype(f32) for a in range(3))
        at = b * c1
        for rows, a, value in (
            (0, 0, first + second),
            (0, 1, third),
            (1, 0, first),
            (1, 1, second + third),
        ):
            out_up[rows * c2 : (rows + 1) * c2, a * 3 * c1 + at : a * 3 * c1 + at + c1] = (
                value.astype(bf16)
            )
    out_fine[...] = jnp.zeros(out_fine.shape, bf16)
    for t in range(3):
        for a in range(3):
            for b in range(3):
                block = fine[t, a, b]
                for rho in range(2):
                    at = ((a + rho) * 3 + b) * c2
                    out_fine[t, rho * c2 : (rho + 1) * c2, at : at + c2] = block


CHUNKS = 4


def fold(ref, line):
    channels, width = line.shape
    ref[:channels] = line[:, : width // 2]
    ref[channels:] = line[:, width // 2 :]


def unfold(ref):
    channels = ref.shape[0] // 2
    return jnp.concatenate([ref[:channels], ref[channels:]], axis=1)


def fetches(source, target, arrived):
    part = source.shape[0] // CHUNKS
    cuts = [pl.ds(k * part, part) for k in range(CHUNKS)]
    return [
        pltpu.make_async_copy(source.at[cut], target.at[cut], arrived.at[k])
        for k, cut in enumerate(cuts)
    ]


def turn_kernel(
    latent, cache, fine, lat_t, cache_t, send, fine_v, lat_v, cache_v, lat_in, cache_in, fine_in
):
    lat_copies = fetches(latent, lat_v, lat_in)
    cache_copies = fetches(cache, cache_v, cache_in)
    fine_copies = fetches(fine, fine_v, fine_in)
    for copy in lat_copies + cache_copies + fine_copies:
        copy.start()
    for copy in lat_copies:
        copy.wait()
    lat_t[...] = jnp.swapaxes(lat_v[...], 0, 1)
    for copy in cache_copies:
        copy.wait()
    cache_t[...] = jnp.swapaxes(cache_v[...], 0, 1)

    @pl.when(lax.axis_index("tm") == 0)
    def _():
        send[...] = lat_t[...]

    @pl.when(lax.axis_index("tm") != 0)
    def _():
        send[...] = cache_t[...]

    for copy in fine_copies:
        copy.wait()


def moments_kernel(lat_t, cache_t, fine, pay, fine_t, up, down):
    rows, _, width = lat_t.shape
    fine_t[...] = jnp.swapaxes(fine[...], 0, 1)
    for ref, cut, line in (
        (up, slice(rows - 2, rows), fine_t[2 * rows - 1]),
        (down, slice(0, 2), fine_t[0]),
    ):
        ref[0:2] = lat_t[cut]
        ref[2:4] = cache_t[cut]
        fold(ref.at[4], line)
    payload(pay, *moments([lat_t[r] for r in range(rows)], rows * width))


def coarse_first(cache_t, above, below, weights, acc, stack):
    rows, channels, width = cache_t.shape
    for r in range(2):
        put(stack, 0, r, above[2 + r])
        put(stack, 0, rows + 2 + r, below[2 + r])
    for r in range(rows):
        put(stack, 0, 2 + r, cache_t[r])
    step = 3 * channels
    for r in range(rows + 2):
        acc[r] = dot(weights[0], stack[0, r * step : (r + 3) * step])


def put_normed(stack, middle, above, below, stats, frame, gain, shift):
    tile = lax.axis_index("tile")
    last = lax.axis_size("tile") - 1
    rows, (channels, width) = len(middle), middle[0].shape
    centre, spread = combine(stats, frame, channels, rows * width)
    scale, offset = spread * column(gain), column(shift)
    top = jnp.where(tile == 0, 0.0, 1.0)
    bottom = jnp.where(tile == last, 0.0, 1.0)
    for r in range(2):
        put(stack, 0, r, silu_norm(above[r], centre, scale, offset) * top)
        put(stack, 0, rows + 2 + r, silu_norm(below[r], centre, scale, offset) * bottom)
    for r in range(rows):
        put(stack, 0, 2 + r, silu_norm(middle[r], centre, scale, offset))


def rows_of(*refs):
    return [ref.at[r] for ref in refs for r in range(ref.shape[0])]


def coarse_third(lat_t, above, below, stats, gain, shift, weights, acc, out, stack):
    frame = lax.axis_index("tm")
    put_normed(
        stack, rows_of(lat_t), rows_of(above), rows_of(below), stats, frame, gain, shift
    )
    rows, channels, _ = lat_t.shape
    step = 3 * channels
    for r in range(rows + 2):
        out[r] = acc[r] + dot(weights[2], stack[0, r * step : (r + 3) * step])


def coarse_second(
    other, above, below, stats, gain, shift, weights, acc, out, rims, stack
):
    frame = lax.axis_index("tm")
    tile = lax.axis_index("tile")
    last = lax.axis_size("tile") - 1
    rows, channels, _ = other.shape
    other, above, below = rows_of(other), rows_of(above), rows_of(below)

    @pl.when(frame == 0)
    def _():
        for r, ref in enumerate(above + other + below):
            put(stack, 0, r, ref[...])

    @pl.when(frame != 0)
    def _():
        put_normed(stack, other, above, below, stats, 0, gain, shift)

    step = 3 * channels
    for r in range(rows + 2):
        value = acc[r] + dot(weights[1], stack[0, r * step : (r + 3) * step])
        if r == 0:
            value = value * jnp.where(tile == 0, 0.0, 1.0)
        if r == rows + 1:
            value = value * jnp.where(tile == last, 0.0, 1.0)
        target = rims.at[r // rows] if r in (0, rows + 1) else out.at[r - 1]
        target[...] = value.astype(bf16)


def raise_rows(coarse, weights, raised, stack):
    rows, (channels, width) = len(coarse), coarse[0].shape
    row = lax.broadcasted_iota(jnp.int32, (width, 2 * width), 0)
    col = lax.broadcasted_iota(jnp.int32, (width, 2 * width), 1) // 2
    spread_out = (row == col).astype(f32).astype(bf16)
    for r in range(rows):
        put(stack, 0, r, dot(coarse[r][...], spread_out))
    step = 3 * channels
    c2 = weights.shape[0] // 2
    for m in range(rows - 1):
        both = dot(weights[...], stack[0, m * step : (m + 2) * step]).astype(bf16)
        raised[2 * m] = both[:c2]
        raised[2 * m + 1] = both[c2:]


def up_kernel(coarse, rims, above, below, weights, raised, pay, late, stack):
    frame = lax.axis_index("tm")

    @pl.when(frame == 0)
    def _():
        late[...] = rims[...]

    @pl.when(frame != 0)
    def _():
        late[0] = above[4]
        late[1] = below[4]

    raise_rows([rims.at[0], *rows_of(coarse), rims.at[1]], weights, raised, stack)
    count = raised.shape[0] - 2
    payload(pay, *moments([raised[r + 1] for r in range(count)], count * raised.shape[2]))


def put_active(stack, raised, stats, frame, gain, shift):
    tile = lax.axis_index("tile")
    last = lax.axis_size("tile") - 1
    rows, (channels, width) = len(raised), raised[0].shape
    centre, spread = combine(stats, frame, channels, (rows - 2) * width)
    scale, offset = spread * column(gain), column(shift)
    for r in range(rows):
        value = silu_norm(raised[r], centre, scale, offset)
        if r == 0:
            value = value * jnp.where(tile == 0, 0.0, 1.0)
        if r == rows - 1:
            value = value * jnp.where(tile == last, 0.0, 1.0)
        put(stack, 0, r, value)


def put_rims(stack, last, above, below):
    put(stack, 0, 0, unfold(above))
    put(stack, 0, last, unfold(below))


def put_cache(stack, fine_t):
    for r in range(fine_t.shape[0]):
        put(stack, 0, 1 + r, fine_t[r])


def fine_window(stack, m, step):
    return stack[0, 2 * m * step : (2 * m + 4) * step]


def fine_first(fine_t, above, below, weights, acc, stack):
    put_rims(stack, fine_t.shape[0] + 1, above.at[4], below.at[4])
    put_cache(stack, fine_t)
    for m in range(acc.shape[0]):
        acc[m] = dot(weights[0], fine_window(stack, m, 3 * fine_t.shape[1]))


def fine_third(raised, stats, gain, shift, weights, acc, out, stack):
    put_active(stack, rows_of(raised), stats, lax.axis_index("tm"), gain, shift)
    for m in range(acc.shape[0]):
        out[m] = acc[m] + dot(weights[2], fine_window(stack, m, 3 * raised.shape[1]))


def fine_begin(fine_r, coarse, weights, raised, stack, stack_up):
    frame = lax.axis_index("tm")

    @pl.when(frame == 0)
    def _():
        put_cache(stack, fine_r)

    @pl.when(frame != 0)
    def _():
        raise_rows(rows_of(coarse), weights, raised, stack_up)


def fine_end(begun, coarse, late, raised, stats, gain, shift, weights, stack, ends, stack_up):
    frame = lax.axis_index("tm")

    @pl.when(frame == 0)
    def _():
        put_rims(stack, 2 * coarse.shape[0] + 1, late.at[0], late.at[1])

    @pl.when(frame != 0)
    def _():
        top, bottom = ends.at[0:2], ends.at[2:4]
        raise_rows([late.at[0], coarse.at[0]], weights, top, stack_up)
        raise_rows([coarse.at[coarse.shape[0] - 1], late.at[1]], weights, bottom, stack_up)
        put_active(stack, rows_of(top, raised, bottom), stats, 0, gain, shift)


def fine_second(stack, bias, weights, acc, out, turned):
    c2 = out.shape[0]
    offset = column(bias)
    for m in range(acc.shape[0]):
        both = acc[m] + dot(weights[1], fine_window(stack, m, 3 * c2))
        turned[2 * m] = (both[:c2] + offset).astype(bf16)
        turned[2 * m + 1] = (both[c2:] + offset).astype(bf16)
    out[...] = jnp.swapaxes(turned[...], 0, 1)


def per_device(
    latent,
    coarse_cache,
    fine_cache,
    gain_coarse,
    shift_coarse,
    weight_coarse,
    weight_up,
    gain_fine,
    shift_fine,
    weight_fine,
    bias_fine,
):
    _, c1, rows, cols = latent.shape
    c2 = fine_cache.shape[1]
    tiles = lax.axis_size("tile")
    fine_rows, fine_cols = 2 * rows, 2 * cols
    forward = [(i, i + 1) for i in range(tiles - 1)]
    backward = [(i + 1, i) for i in range(tiles - 1)]
    later, earlier = [(0, 1)], [(1, 0)]
    gain_coarse, shift_coarse = gain_coarse[None], shift_coarse[None]
    gain_fine, shift_fine, bias_fine = gain_fine[None], shift_fine[None], bias_fine[None]

    def shared(stats):
        return lax.all_to_all(stats, ("tm", "tile"), 0, 0)

    def after(value, *others):
        return lax.optimization_barrier((value, *others))[0]

    devices = lax.axis_size("tm") * tiles
    coarse_shape, coarse_acc = (rows, c1, cols), ((rows + 2, c1, cols), f32)
    fine_acc = ((rows, 2 * c2, fine_cols), f32)
    coarse_stack = pltpu.VMEM((1, (rows + 4) * 3 * c1, cols), bf16)
    stack_shape = ((1, (fine_rows + 2) * 3 * c2, fine_cols), bf16)
    fine_scratch = pltpu.VMEM(*stack_shape)
    up_stack = pltpu.VMEM((1, (rows + 2) * 3 * c1, fine_cols), bf16)
    raised_shape = ((fine_rows + 2, c2, fine_cols), bf16)

    rim = ((5, c1, cols), bf16)
    fine_raw = ((c2, fine_rows, fine_cols), bf16)
    lat_t, cache_t, send, fine_v = call(
        turn_kernel,
        "turn",
        [(coarse_shape, bf16)] * 3 + [fine_raw],
        [pltpu.VMEM((c1, rows, cols), bf16)] * 2 + [pltpu.SemaphoreType.DMA((CHUNKS,))] * 3,
        far=3,
    )(latent[0], coarse_cache[0], fine_cache[0])
    other = lax.ppermute(send, "tm", [(0, 1), (1, 0)])
    pay, fine_t, rim_up, rim_down = call(
        moments_kernel,
        "moments",
        [((devices, 1, 4 * GROUPS), f32), ((fine_rows, c2, fine_cols), bf16)] + [rim] * 2,
    )(lat_t, cache_t, fine_v)
    above = lax.ppermute(rim_up, "tile", forward)
    below = lax.ppermute(rim_down, "tile", backward)
    w_coarse, w_up, w_fine = call(
        weights_kernel,
        "weights",
        [((3, c1, 9 * c1), bf16), ((2 * c2, 6 * c1), bf16), ((3, 2 * c2, 12 * c2), bf16)],
    )(weight_coarse, weight_up, weight_fine)
    stats = shared(after(pay, w_coarse))
    stats, other, above, below = lax.optimization_barrier((stats, other, above, below))
    (acc_first,) = call(coarse_first, "coarse_first", [coarse_acc], [coarse_stack])(
        cache_t, above, below, w_coarse
    )
    other_above = lax.ppermute(other[rows - 2 :], "tile", forward)
    other_below = lax.ppermute(other[:2], "tile", backward)
    (acc,) = call(coarse_third, "coarse_third", [coarse_acc], [coarse_stack])(
        lat_t,
        above,
        below,
        stats,
        gain_coarse,
        shift_coarse,
        w_coarse,
        after(acc_first, other_above, other_below),
    )
    fine_r = lax.ppermute(after(fine_t, acc_first, other_above, other_below), "tm", earlier)
    coarse, coarse_rims = call(
        coarse_second,
        "coarse_second",
        [(coarse_shape, bf16), ((2, c1, cols), bf16)],
        [coarse_stack],
    )(other, other_above, other_below, stats, gain_coarse, shift_coarse, w_coarse, acc)
    coarse_r = lax.ppermute(coarse, "tm", later)
    raised, pay, late = call(
        up_kernel,
        "up",
        [raised_shape, ((devices, 1, 4 * GROUPS), f32), ((2, c1, cols), bf16)],
        [up_stack],
    )(coarse, coarse_rims, above, below, w_up)
    (acc,) = call(fine_first, "fine_first", [fine_acc], [fine_scratch])(
        fine_t, above, below, w_fine
    )

    stats = shared(after(pay, acc))
    stats, fine_r, coarse_r = lax.optimization_barrier((stats, fine_r, coarse_r))
    late = lax.ppermute(after(late, stats), "tm", [(0, 1), (1, 0)])
    raised_r, stack = call(
        fine_begin,
        "fine_begin",
        [((fine_rows - 2, c2, fine_cols), bf16), stack_shape],
        [up_stack],
    )(fine_r, coarse_r, w_up)
    (acc,) = call(fine_third, "fine_third", [fine_acc], [fine_scratch])(
        raised, stats, gain_fine, shift_fine, w_fine, acc
    )
    (stack,) = call(
        fine_end,
        "fine_end",
        [stack_shape],
        [pltpu.VMEM((4, c2, fine_cols), bf16), up_stack],
        aliases={0: 0},
    )(stack, coarse_r, late, raised_r, stats, gain_fine, shift_fine, w_up)
    (out,) = call(
        fine_second,
        "fine_second",
        [fine_raw],
        [pltpu.VMEM((fine_rows, c2, fine_cols), bf16)],
        local=False,
    )(stack, bias_fine, w_fine, acc)
    return out[None]


def solution(mesh):
    split = P("tm", None, "tile", None)
    return jax.shard_map(
        per_device,
        mesh=mesh,
        in_specs=(split,) * 3 + (P(),) * 8,
        out_specs=split,
        check_vma=False,
    )
```
